512 devices in a mesh: gx: 8 (over z), gy: 4 (over x), gz: 16 (over y, core).
Axes of the slice: x: 4, y: 8, z: 8, core: 2. Of those that a mesh axis runs over, the one named last changes fastest.
Arguments:
- body_forces: float32 [3, 64, 32, 2048], P(None, 'gx', 'gy', 'gz'), may hold values from -8 to 8, as said below
- material: int32 [64, 32, 2048], P('gx', 'gy', 'gz'), may hold values from 0 to 15
- fixed_mask: int32 [64, 32, 2048], P('gx', 'gy', 'gz'), may hold values 0 or 1
- moduli: float32 [2, 16], replicated, may hold values from 0.05 to 1
Outputs:
- displacement: float32 [3, 64, 32, 2048], P(None, 'gx', 'gy', 'gz')
- residual: float32 [3, 64, 32, 2048], P(None, 'gx', 'gy', 'gz')
The draws below stay inside these ranges and needn't reach their ends.
Inputs may be any that keep to these rules, and one draw needn't show every extreme that they name: `body_forces`: forces on the voxels, of order one.
All inputs are finite; a program needn't handle non-finite values. No bound on the sum of `fixed_mask` on one device may be relied on, other than what follows from the above.
Results may differ from the reference program's by a relative error of at most 0.0001.
Values sent between devices are 32-bit elements; how exact they have to be, the bound alone decides.
No kernel may reach another device: no remote copies, remote signals or barrier semaphores. Data moves between devices by JAX's collectives and lax.ppermute only.
A program may use at most 128 MiB of HBM per device.

```python
import math
import jax
import jax.numpy as jnp
from jax import lax

SMOOTH = 4
AGX = 1
AGY = 1
AGZ = 16
CLASSES = 16
NX = 64
NY = 32
NZ = 2048


def draw_body_forces(key, part):
    shape_full = (3, NX, NY, NZ)
    return jax.random.truncated_normal(key, -6.0, 6.0, shape_full, jnp.float32)


def with_ends(entries, rng, smallest, largest):
    place = [jax.random.randint(jax.random.fold_in(rng, axis), (), 0, length) for axis, length in enumerate(entries.shape)]
    widest = entries.shape.index(max(entries.shape))
    neighbour = place[:widest] + [(place[widest] + 1) % entries.shape[widest]] + place[widest + 1:]
    return entries.at[tuple(place)].set(smallest).at[tuple(neighbour)].set(largest)


def setup_inputs(seed: int = 0) -> dict:
    key_list = jax.random.split(jax.random.key(seed), 5)
    return {
        "body_forces": draw_body_forces(jax.random.fold_in(key_list[4], 71), 0),
        "material": with_ends(jax.random.randint(key_list[1], (NX, NY, NZ), 0, CLASSES), jax.random.fold_in(key_list[1], 1), 0, CLASSES - 1).astype(jnp.int32),
        "fixed_mask": with_ends((jax.random.randint(key_list[2], (NX, NY, NZ), 0, 8) < 1).astype(jnp.int32), jax.random.fold_in(key_list[2], 1), 0, 1),
        "moduli": jnp.clip(jnp.exp(jax.random.uniform(key_list[3], (2, CLASSES), jnp.float32, math.log(0.05), math.log(1.0))), 0.05, 1.0),
    }


CHEB_CENTER = 1.125
CHEB_HALF = 0.875

def coarsen(values, factor_x, factor_y, factor_z, method):
    leading = values.shape[:-3]
    size_x, size_y, size_z = values.shape[-3:]
    blocks = values.reshape(leading + (size_x // factor_x, factor_x, size_y // factor_y, factor_y, size_z // factor_z, factor_z))
    offset = len(leading)
    summed_axes = (offset + 1, offset + 3, offset + 5)
    if method == 'mean':
        return jnp.mean(blocks, axis=summed_axes)
    if method == 'most':
        return jnp.max(blocks, axis=summed_axes)
    return jnp.sum(blocks, axis=summed_axes)

def prolong(values, factor_x, factor_y, factor_z):
    return jnp.repeat(jnp.repeat(jnp.repeat(values, factor_x, axis=-3), factor_y, axis=-2), factor_z, axis=-1)

def pad_zero(values):
    return jnp.pad(values, ((0, 0), (1, 1), (1, 1), (1, 1)))

def prepare(material_now, active, scales, pad_material):
    padded = pad_material(material_now)
    face_vals = (0.5 * scales[0] * (padded[:, :-1, 1:-1, 1:-1] + padded[:, 1:, 1:-1, 1:-1]), 0.5 * scales[1] * (padded[:, 1:-1, :-1, 1:-1] + padded[:, 1:-1, 1:, 1:-1]), 0.5 * scales[2] * (padded[:, 1:-1, 1:-1, :-1] + padded[:, 1:-1, 1:-1, 1:]))
    coefficients = []
    diagonals = []
    for component in range(3):
        stiff_row = []
        summed = jnp.zeros(active.shape, jnp.float32)
        for direction in range(3):
            facing = face_vals[direction]
            if component == direction:
                stiffness = facing[0] + (facing[1] + facing[0])
            else:
                stiffness = facing[0]
            length = active.shape[direction]
            summed = summed + lax.slice_in_dim(stiffness, 0, length, axis=direction) + lax.slice_in_dim(stiffness, 1, length + 1, axis=direction)
            stiff_row.append(stiffness)
        coefficients.append(stiff_row)
        diagonals.append(summed)
    diagonal = jnp.stack(diagonals)
    inverse = 1.0 / (active * diagonal + (1.0 - active))
    return (coefficients, diagonal, active, inverse)

def operate(values, level_data, pad_field):
    coefficients, diagonal, active, inverse = level_data
    masked = active * values
    padded = pad_field(masked)
    results = []
    for component in range(3):
        component_field = padded[component]
        summed = diagonal[component] * masked[component]
        neighbours = ((component_field[:-2, 1:-1, 1:-1], component_field[2:, 1:-1, 1:-1]), (component_field[1:-1, :-2, 1:-1], component_field[1:-1, 2:, 1:-1]), (component_field[1:-1, 1:-1, :-2], component_field[1:-1, 1:-1, 2:]))
        for direction in range(3):
            stiffness = coefficients[component][direction]
            length = masked.shape[1 + direction]
            lower_faces = lax.slice_in_dim(stiffness, 0, length, axis=direction)
            upper_faces = lax.slice_in_dim(stiffness, 1, length + 1, axis=direction)
            summed = summed - lower_faces * neighbours[direction][0] - upper_faces * neighbours[direction][1]
        results.append(summed)
    return active * jnp.stack(results) + (1.0 - active) * values

def smooth(solution, residual, level_data, pad_field):
    inverse = level_data[3]
    center_ratio = CHEB_CENTER / CHEB_HALF
    rho_now = 1.0 / center_ratio
    update = inverse * residual / CHEB_CENTER
    for sweep_index in range(3):
        solution = solution + update
        residual = residual - operate(update, level_data, pad_field)
        if sweep_index < 2:
            rho_next = 1.0 / (2.0 * center_ratio - rho_now)
            update = rho_next * rho_now * update + 2.0 * rho_next / CHEB_HALF * inverse * residual
            rho_now = rho_next
    return (solution, residual)

def assemble(level_data):
    coefficients, diagonal, active, inverse = level_data
    grid_shape = active.shape
    cell_count = grid_shape[0] * grid_shape[1] * grid_shape[2]
    strides = (grid_shape[1] * grid_shape[2], grid_shape[2], 1)
    positions = jnp.arange(cell_count, dtype=jnp.int32)
    flat_active = active.reshape(cell_count)
    matrices = []
    for component in range(3):
        matrix = jnp.diag(diagonal[component].reshape(cell_count))
        for direction in range(3):
            length = grid_shape[direction]
            upper_faces = lax.slice_in_dim(coefficients[component][direction], 1, length + 1, axis=direction)
            inside = lax.broadcasted_iota(jnp.int32, grid_shape, direction) < length - 1
            link_values = jnp.where(inside, upper_faces, jnp.zeros_like(upper_faces)).reshape(cell_count)
            pattern = (positions[None, :] == positions[:, None] + strides[direction]).astype(jnp.float32)
            coupling = link_values[:, None] * pattern
            matrix = matrix - coupling - coupling.T
        matrix = flat_active[:, None] * matrix * flat_active[None, :] + jnp.diag(1.0 - flat_active)
        matrices.append(matrix)
    return jnp.stack(matrices)

def coarse_solve(factors, right_side):
    flat_side = right_side.reshape(3, -1)
    solved = jax.vmap(lambda factor, column: jax.scipy.linalg.cho_solve((factor, True), column))(factors, flat_side)
    return solved.reshape(right_side.shape)

def coarse_scales():
    extent_x = float(2 ** (SMOOTH - 1) * AGX)
    extent_y = float(2 ** (SMOOTH - 1) * AGY)
    extent_z = float(2 ** (SMOOTH - 1) * AGZ)
    return (extent_y * extent_z / extent_x, extent_x * extent_z / extent_y, extent_x * extent_y / extent_z)

def run_cycle(depth_now, right_side, level_list, factors):
    level_data = level_list[depth_now]
    solution, residual = smooth(jnp.zeros_like(right_side), right_side, level_data, pad_zero)
    if depth_now + 1 < len(level_list):
        lower_solution, unused = run_cycle(depth_now + 1, coarsen(residual, 2, 2, 2, 'sum'), level_list, factors)
        correction = prolong(lower_solution, 2, 2, 2)
    else:
        coarse_side = coarsen(residual, AGX, AGY, AGZ, 'sum')
        correction = prolong(coarse_solve(factors, coarse_side), AGX, AGY, AGZ)
    solution = solution + correction
    residual = residual - operate(correction, level_data, pad_zero)
    return smooth(solution, residual, level_data, pad_zero)

def reference(body_forces, material, fixed_mask, moduli):
    shear_modulus = jnp.take(moduli[0], material)
    lame_modulus = jnp.take(moduli[1], material)
    material_now = jnp.stack([shear_modulus, lame_modulus])
    active_now = (1 - fixed_mask).astype(jnp.float32)
    level_list = []
    for level_index in range(SMOOTH):
        if level_index > 0:
            material_now = coarsen(material_now, 2, 2, 2, 'mean')
            active_now = coarsen(active_now, 2, 2, 2, 'most')
        level_scale = float(2 ** level_index)
        level_list.append(prepare(material_now, active_now, (level_scale, level_scale, level_scale), pad_zero))
    coarse_level = prepare(coarsen(material_now, AGX, AGY, AGZ, 'mean'), coarsen(active_now, AGX, AGY, AGZ, 'most'), coarse_scales(), pad_zero)
    factors = jnp.linalg.cholesky(assemble(coarse_level))
    displacement, residual = run_cycle(0, body_forces, level_list, factors)
    return (displacement, residual)
```

```python
import jax
import jax.numpy as jnp
from jax import lax
from jax.experimental import pallas as pl
from jax.experimental.pallas import tpu as pltpu
from jax.sharding import PartitionSpec as P

F32 = jnp.float32
CLASSES = 16
THETA = 1.125
HALF = 0.875
SIGMA = THETA / HALF
VMEM_LIMIT = 50 * 1024 * 1024


def cheb_factors():
    rho = 1.0 / SIGMA
    found = []
    for _ in range(2):
        rho_next = 1.0 / (2.0 * SIGMA - rho)
        found.append((rho_next * rho, 2.0 * rho_next / HALF))
        rho = rho_next
    return found


CHEB = cheb_factors()
START = (0.0, 1.0 / THETA)


def dot(a, b):
    return lax.dot_general(
        a, b, (((1,), (0,)), ((), ())), precision=lax.Precision.HIGHEST, preferred_element_type=F32
    )


def dot_nt(a, b):
    return lax.dot_general(
        a, b, (((1,), (1,)), ((), ())), precision=lax.Precision.HIGHEST, preferred_element_type=F32
    )


def iota(shape, dim):
    return lax.broadcasted_iota(jnp.int32, shape, dim)


def ones_where(cond):
    return jnp.where(cond, 1.0, 0.0).astype(F32)


def roll(v, shift, axis):
    size = v.shape[axis]
    return pltpu.roll(v, shift % size, axis)


def neighbours_y(v, rows_masked):
    down, up = roll(v, 1, 0), roll(v, -1, 0)
    if rows_masked:
        row = iota(v.shape, 0)
        down = jnp.where(row >= 1, down, 0.0)
        up = jnp.where(row <= v.shape[0] - 2, up, 0.0)
    return down, up


def plane_factors(mod, scale, faces, diag, inv, lo, hi, rows_masked):
    half = 0.5 * scale

    def body(i, carry):
        def fields(j):
            shear, lame = mod[0, j], mod[1, j]
            return half * shear, half * (shear + lame)

        p, g = fields(i)
        pm, gm = fields(i - 1)
        pp, gp = fields(i + 1)
        a, am = mod[2, i], mod[2, i - 1]
        pyd, pyu = neighbours_y(p, rows_masked)
        gyd, gyu = neighbours_y(g, rows_masked)
        ayd, _ = neighbours_y(a, rows_masked)
        pzd, pzu = roll(p, 1, 1), roll(p, -1, 1)
        gzd, gzu = roll(g, 1, 1), roll(g, -1, 1)
        azd = roll(a, 1, 1)
        base = (pm + pp) + (pyd + pyu) + (pzd + pzu) + 6.0 * p
        extra = (gm + gp, gyd + gyu, gzd + gzu)
        for c in range(3):
            d = a * (base + (extra[c] + 2.0 * g)) + (1.0 - a)
            diag[c, i] = d
            inv[c, i] = 1.0 / d
        for k, (pn, gn, an) in enumerate(((pm, gm, am), (pyd, gyd, ayd), (pzd, gzd, azd))):
            both = a * an
            face = p + pn
            faces[2 * k, i] = both * face
            faces[2 * k + 1, i] = both * (face + (g + gn))
        return carry

    lax.fori_loop(lo, hi, body, 0)


def plane_sweep(d, d_next, r_in, r_out, faces, diag, inv, lo, hi, pair, r_in_at=0, r_out_at=0):
    def body(i, carry):
        for c in range(3):
            fx = faces[1 if c == 0 else 0, i]
            fxu = faces[1 if c == 0 else 0, i + 1]
            fy = faces[3 if c == 1 else 2, i]
            fz = faces[5 if c == 2 else 4, i]
            dc = d[c, i]
            t = fx * d[c, i - 1] + fxu * d[c, i + 1]
            t = t + (fy * roll(dc, 1, 0) + roll(fy * dc, -1, 0))
            t = t + (fz * roll(dc, 1, 1) + roll(fz * dc, -1, 1))
            r = r_in[c, i - r_in_at] - (diag[c, i] * dc - t)
            if r_out is not None:
                r_out[c, i - r_out_at] = r
            if pair is not None:
                new = (pair[1] * inv[c, i]) * r
                if pair[0] != 0.0:
                    new = new + pair[0] * dc
                d_next[c, i] = new
        return carry

    lax.fori_loop(lo, hi, body, 0)


def kernel_a(moduli, ext, send, r_out, x_out, mod, faces, diag, inv, d_a, d_b, r):
    def look_up(i, carry):
        mat = ext[3, i]
        shear = jnp.zeros(mat.shape, F32)
        lame = jnp.zeros(mat.shape, F32)
        for k in range(CLASSES):
            hit = mat == float(k + 1)
            shear = jnp.where(hit, moduli[0, k], shear)
            lame = jnp.where(hit, moduli[1, k], lame)
        mod[0, i] = shear
        mod[1, i] = lame
        mod[2, i] = ext[4, i]
        return carry

    lax.fori_loop(0, 22, look_up, 0)
    plane_factors(mod, 1.0, faces, diag, inv, 1, 21, False)

    def start(i, carry):
        for c in range(3):
            d_a[c, i] = (START[1] * inv[c, i]) * ext[c, i]
        return carry

    lax.fori_loop(1, 21, start, 0)
    plane_sweep(d_a, d_b, ext, r, faces, diag, inv, 2, 20, CHEB[0])
    for c in range(3):
        x_out[c] = d_a[c, 7:15, 0:8, 0:128] + d_b[c, 7:15, 0:8, 0:128]
    plane_sweep(d_b, d_a, r, r, faces, diag, inv, 3, 19, CHEB[1])
    for c in range(3):
        x_out[c] = x_out[c] + d_a[c, 7:15, 0:8, 0:128]
    plane_sweep(d_a, None, r, r_out, faces, diag, inv, 4, 18, None, 0, 4)
    rows = []
    for c in range(3):
        for j in range(4):
            rows.append(r_out[c, 3 + 2 * j, 0:8] + r_out[c, 4 + 2 * j, 0:8])
    for k in range(3):
        for j in range(4):
            rows.append(mod[k, 7 + 2 * j, 0:8] + mod[k, 8 + 2 * j, 0:8])
    stacked = jnp.concatenate(rows, axis=0)
    pair_z = ones_where(iota((256, 128), 0) // 2 == iota((256, 128), 1))
    pair_y = ones_where(iota((96, 192), 1) // 2 == iota((96, 192), 0))
    low = dot(pair_y, dot(stacked, pair_z))
    row = iota((96, 128), 0)
    low = jnp.where(row < 48, low, jnp.where(row < 80, 0.125 * low, ones_where(low > 0.5)))
    send[...] = low


def flat_factors(mods, steps, scales, groups):
    shear, lame, a = mods
    total = 0.0
    faces = []
    for (axis, shift, below, above), scale, share in zip(steps, scales, groups):
        h = (0.5 * scale) * (shear + share * (shear + lame))
        dn, up = roll(h, shift, axis), roll(h, -shift, axis)
        an = roll(a, shift, axis)
        if below is not None:
            dn = jnp.where(below, dn, 0.0)
            up = jnp.where(above, up, 0.0)
            an = jnp.where(below, an, 0.0)
        total = total + (2.0 * h + (dn + up))
        faces.append((a * an) * (h + dn))
    diag = a * total + (1.0 - a)
    return faces, diag, 1.0 / diag


def flat_apply(v, factors, steps):
    faces, diag, inv = factors
    out = diag * v
    for face, (axis, shift, below, above) in zip(faces, steps):
        out = out - (face * roll(v, shift, axis) + roll(face * v, -shift, axis))
    return out


def flat_smooth(x, r, factors, steps, last):
    inv = factors[2]
    d = (START[1] * inv) * r
    for sweep in range(3):
        x = d if x is None else x + d
        if sweep == 2 and not last:
            return x, None
        r = r - flat_apply(d, factors, steps)
        if sweep < 2:
            c1, c2 = CHEB[sweep]
            d = c1 * d + (c2 * inv) * r
    return x, r


def level2_steps():
    lane = iota((64, 128), 1)
    return (
        (1, 8, lane >= 8, lane < 120),
        (1, 1, lane % 8 >= 1, lane % 8 <= 6),
        (0, 1, None, None),
    )


def level3_steps(rows):
    lane = iota((rows, 128), 1)
    row = iota((rows, 128), 0)
    return (
        (1, 4, lane % 32 >= 4, lane % 32 < 28),
        (1, 1, lane % 4 >= 1, lane % 4 <= 2),
        (0, 1, row >= 1, row <= rows - 2),
    )


def level3_groups(rows):
    group = iota((rows, 128), 1) // 32
    return tuple(ones_where(group == k) for k in range(3))


def to_level3(k):
    cell = iota((128, 128), 0)
    lane = iota((128, 128), 1)
    return ones_where(lane == 32 * k + (cell // 16) * 4 + (cell % 8) // 2)


def kernel_b(got, send, mod1, x1, r1, mod2, x2, r2, faces, diag, inv, d_a, d_b, b1):
    sub = iota((8, 128), 0) < 4
    zero = jnp.zeros((16, 128), F32)
    for k in range(3):
        mod1[k, 0] = zero
        mod1[k, 33] = zero
        d_a[k, 0] = zero
        d_a[k, 33] = zero
        d_b[k, 0] = zero
        d_b[k, 33] = zero
    for k in range(6):
        faces[k, 33] = zero

    def unpack(gx, carry):
        for f in range(6):
            for pair in range(2):
                at = f * 16 + pair * 8
                for half in range(2):
                    s0 = got[gx * 4 + 2 * half, at : at + 8]
                    s1 = got[gx * 4 + 2 * half + 1, at : at + 8]
                    even = jnp.where(sub, s0, roll(s1, 4, 0))
                    odd = jnp.where(sub, roll(s0, 4, 0), s1)
                    x = gx * 4 + 2 * pair + 1
                    rows = slice(8 * half, 8 * half + 8)
                    if f < 3:
                        b1[f, x, rows] = even
                        b1[f, x + 1, rows] = odd
                    else:
                        mod1[f - 3, x, rows] = even
                        mod1[f - 3, x + 1, rows] = odd
        return carry

    lax.fori_loop(0, 8, unpack, 0)
    plane_factors(mod1, 2.0, faces, diag, inv, 1, 33, True)

    def start(i, carry):
        for c in range(3):
            d_a[c, i] = (START[1] * inv[c, i]) * b1[c, i]
        return carry

    lax.fori_loop(1, 33, start, 0)
    plane_sweep(d_a, d_b, b1, r1, faces, diag, inv, 1, 33, CHEB[0])
    for c in range(3):
        x1[c] = d_a[c] + d_b[c]
    plane_sweep(d_b, d_a, r1, r1, faces, diag, inv, 1, 33, CHEB[1])
    for c in range(3):
        x1[c] = x1[c] + d_a[c]
    plane_sweep(d_a, None, r1, r1, faces, diag, inv, 1, 33, None)

    pair_y = ones_where(iota((128, 256), 1) // 2 == iota((128, 256), 0))
    pair_z = ones_where(iota((64, 128), 1) // 2 == iota((64, 128), 0))

    def restrict(ref, k):
        planes = [ref[k, 1 + 2 * j] + ref[k, 2 + 2 * j] for j in range(16)]
        return dot_nt(pair_z, dot(pair_y, jnp.concatenate(planes, axis=0)))

    shear = 0.125 * restrict(mod1, 0)
    lame = 0.125 * restrict(mod1, 1)
    active = ones_where(restrict(mod1, 2) > 0.5)
    mod2[0] = shear
    mod2[1] = lame
    mod2[2] = active
    steps = level2_steps()
    own_z = ones_where(iota((16, 64), 1) // 2 == iota((16, 64), 0))
    low = jnp.zeros((16, 128), F32)
    for c in range(3):
        shares = tuple(1.0 if c == k else 0.0 for k in range(3))
        factors = flat_factors((shear, lame, active), steps, (4.0, 4.0, 4.0), shares)
        x, r = flat_smooth(None, restrict(r1, c), factors, steps, True)
        x2[c] = x
        r2[c] = r
        low = low + dot(dot(own_z, r), to_level3(c))
    send[0] = low
    lane = iota((16, 128), 1)
    low = dot(dot(own_z, shear), to_level3(0)) + dot(dot(own_z, lame), to_level3(1))
    low = 0.125 * low
    low = low + ones_where(dot(dot(own_z, active), to_level3(2)) > 0.5)
    send[1] = low


def spread(v, group):
    lane = iota(v.shape, 1)
    v = jnp.where(lane // 32 == group, v, 0.0)
    back = roll(v, -32 * group, 1)
    return back + roll(back, 32, 1) + roll(back, 64, 1)


def coarse_solve(mods3, rest, mat):
    blocks = ones_where(iota((16, 256), 1) // 16 == iota((16, 256), 0))
    shear = 0.0625 * dot(blocks, mods3[0])
    lame = 0.0625 * dot(blocks, mods3[1])
    active = ones_where(dot(blocks, mods3[2]) > 0.5)
    side = dot(blocks, rest)
    steps = level3_steps(16)
    scales = (128.0, 128.0, 0.5)
    faces, diag, _ = flat_factors((shear, lame, active), steps, scales, level3_groups(16))
    columns = [diag, side]
    for face, (axis, shift, below, above) in zip(faces, steps):
        columns.append(face)
        columns.append(jnp.where(above, roll(face, -shift, axis), 0.0))
    stacked = jnp.concatenate(columns, axis=0).T
    row = iota((32, 128), 0)
    lane = iota((32, 128), 1)
    patterns = (
        ones_where(lane == row),
        ones_where(lane == 96),
        -ones_where((lane == row - 4) & (lane < 32)),
        -ones_where((lane == row + 4) & (lane < 32)),
        -ones_where((lane == row - 1) & (lane < 32)),
        -ones_where((lane == row + 1) & (lane < 32)),
        -ones_where(lane == row + 32),
        -ones_where(lane == row + 64),
    )
    for c in range(3):
        part = stacked[32 * c : 32 * c + 32]
        for k in range(16):
            m = 0.0
            for q in range(8):
                at = 16 * q + k
                m = m + part[:, at : at + 1] * patterns[q]
            mat[c, k] = m

    def eliminate(cells):
        a = jnp.stack([mat[c, k] for c, k in cells])
        rows = iota(a.shape, 1)
        for p in range(32):
            pivot = a[:, p : p + 1, :]
            pivot = pivot * (1.0 / a[:, p : p + 1, p : p + 1])
            a = jnp.where(rows == p, pivot, a - a[:, :, p : p + 1] * pivot)
        for n, (c, k) in enumerate(cells):
            mat[c, k] = a[n]

    lane_t = lane < 32
    lane_l = (lane >= 32) & (lane < 64)
    lane_r = (lane >= 64) & (lane < 96)
    lane_b = lane >= 96
    keep = lane_t | lane_b
    none = jnp.zeros((32, 128), F32)
    for h in (1, 2, 4, 8):
        eliminate([(c, k) for c in range(3) for k in range(h, 16, 2 * h)])
        for c in range(3):
            for k in range(0, 16, 2 * h):
                m = mat[c, k]
                left, right = none, none
                if k - h >= 0:
                    w = mat[c, k - h]
                    left = jnp.where(lane_t, roll(w, 64, 1), jnp.where(lane_l | lane_b, w, 0.0))
                if k + h < 16:
                    w = mat[c, k + h]
                    right = jnp.where(lane_t, roll(w, 96, 1), jnp.where(lane_r | lane_b, w, 0.0))
                change = dot(m, jnp.concatenate([none, left, right, none], axis=0))
                mat[c, k] = jnp.where(keep, m, 0.0) - change
    eliminate([(c, 0) for c in range(3)])
    picked = lane == 96
    first_row = ones_where(row == 0)
    pieces = []
    for c in range(3):
        found = {}
        last = jnp.where(picked, mat[c, 0], 0.0)
        found[0] = jnp.broadcast_to(jnp.sum(last, axis=1, keepdims=True), (32, 128))
        for h in (8, 4, 2, 1):
            for k in range(h, 16, 2 * h):
                after = -found[k + h] if k + h < 16 else none
                v = jnp.concatenate([none, -found[k - h], after, first_row], axis=0)
                found[k] = dot(mat[c, k], v)
        piece = none
        for k in range(16):
            piece = jnp.where(lane == k, found[k], piece)
        pieces.append(piece)
    pieces.append(none)
    whole = jnp.concatenate(pieces, axis=0)
    again = ones_where(iota((256, 128), 0) // 16 == iota((256, 128), 1))
    return dot_nt(again, whole)


def kernel_c(
    place, got, mod1, x1, r1, mod2, x2, r2, mod0, x0, r0, disp, resid,
    mat, e3, e1, faces1, diag1, inv1, d1a, d1b, r1w, faces, diag, inv, d_a, d_b, r_w,
):
    gx, gy, gz = place[0], place[1], place[2]
    b3 = jnp.concatenate([got[k, 0] for k in range(16)], axis=0)
    m3 = jnp.concatenate([got[k, 1] for k in range(16)], axis=0)
    mods3 = tuple(spread(m3, k) for k in range(3))
    steps = level3_steps(256)
    factors = flat_factors(mods3, steps, (8.0, 8.0, 8.0), level3_groups(256))
    x, r = flat_smooth(None, b3, factors, steps, True)
    corr = coarse_solve(mods3, r, mat)
    x = x + corr
    r = r - flat_apply(corr, factors, steps)
    x, _ = flat_smooth(x, r, factors, steps, False)
    e3[0:8] = jnp.zeros((8, 128), F32)
    e3[264:272] = jnp.zeros((8, 128), F32)
    e3[8:264] = x
    base = pl.multiple_of(gz * 16, 16)
    own = e3[pl.ds(base + 8, 24)]
    before = e3[pl.ds(base, 8)]
    slab = jnp.concatenate([own, before], axis=0)
    slab = dot(ones_where(iota((64, 32), 0) // 2 == iota((64, 32), 1)), slab)
    steps = level2_steps()
    mods = (mod2[0], mod2[1], mod2[2])
    for k in range(3):
        e1[k, 0] = jnp.zeros((16, 128), F32)
        e1[k, 33] = jnp.zeros((16, 128), F32)
        d1a[k, 0] = jnp.zeros((16, 128), F32)
        d1a[k, 33] = jnp.zeros((16, 128), F32)
        d1b[k, 0] = jnp.zeros((16, 128), F32)
        d1b[k, 33] = jnp.zeros((16, 128), F32)
    for k in range(6):
        faces1[k, 33] = jnp.zeros((16, 128), F32)
    up_xy = ones_where(
        ((iota((512, 128), 0) // 32) * 8 + (iota((512, 128), 0) % 16) // 2) == iota((512, 128), 1)
    )
    up_z = ones_where(iota((64, 128), 1) // 2 == iota((64, 128), 0))
    for c in range(3):
        shares = tuple(1.0 if c == k else 0.0 for k in range(3))
        factors = flat_factors(mods, steps, (4.0, 4.0, 4.0), shares)
        corr = dot_nt(slab, to_level3(c))
        x = x2[c] + corr
        r = r2[c] - flat_apply(corr, factors, steps)
        x, _ = flat_smooth(x, r, factors, steps, False)
        lifted = dot(up_xy, dot(x.T, up_z))
        for j in range(32):
            e1[c, j + 1] = lifted[16 * j : 16 * j + 16]
    plane_factors(mod1, 2.0, faces1, diag1, inv1, 1, 33, True)
    plane_sweep(e1, d1a, r1, r1w, faces1, diag1, inv1, 1, 33, START)
    for c in range(3):
        e1[c, 1:33] = e1[c, 1:33] + x1[c, 1:33] + d1a[c, 1:33]
    plane_sweep(d1a, d1b, r1w, r1w, faces1, diag1, inv1, 1, 33, CHEB[0])
    for c in range(3):
        e1[c, 1:33] = e1[c, 1:33] + d1b[c, 1:33]
    plane_sweep(d1b, d1a, r1w, None, faces1, diag1, inv1, 1, 33, CHEB[1])
    for c in range(3):
        e1[c, 1:33] = e1[c, 1:33] + d1a[c, 1:33]
    row = iota((24, 16), 0)
    row = jnp.where(row >= 16, row - 24, row)
    up_y = ones_where((row + 8 * gy + 16) // 2 - 8 == iota((24, 16), 1))
    up_z0 = ones_where(iota((128, 256), 1) // 2 == iota((128, 256), 0))
    for c in range(3):
        for j in range(8):
            at = jnp.clip(4 * gx + (j - 1), 0, 33)
            lifted = dot(dot(up_y, e1[c, at]), up_z0)
            d_b[c, 3 + 2 * j] = lifted
            d_b[c, 4 + 2 * j] = lifted
    plane_factors(mod0, 1.0, faces, diag, inv, 4, 19, False)
    own_part = (slice(7, 15), slice(0, 8), slice(0, 128))
    for c in range(3):
        disp[c] = x0[c] + d_b[(c,) + own_part]
    plane_sweep(d_b, d_a, r0, r_w, faces, diag, inv, 4, 18, START, 4, 0)
    for c in range(3):
        disp[c] = disp[c] + d_a[(c,) + own_part]
    plane_sweep(d_a, d_b, r_w, r_w, faces, diag, inv, 5, 17, CHEB[0])
    for c in range(3):
        disp[c] = disp[c] + d_b[(c,) + own_part]
    plane_sweep(d_b, d_a, r_w, r_w, faces, diag, inv, 6, 16, CHEB[1])
    for c in range(3):
        disp[c] = disp[c] + d_a[(c,) + own_part]
    plane_sweep(d_a, None, r_w, r_w, faces, diag, inv, 7, 15, None)
    for c in range(3):
        resid[c] = r_w[(c,) + own_part]


IN_VMEM = pl.BlockSpec(memory_space=pltpu.VMEM)
IN_SMEM = pl.BlockSpec(memory_space=pltpu.SMEM)


def shaped(*shape):
    return jax.ShapeDtypeStruct(shape, F32)


def scratch(*shape):
    return pltpu.VMEM(shape, F32)


PARAMS = dict(compiler_params=pltpu.CompilerParams(vmem_limit_bytes=VMEM_LIMIT))


def call_a(moduli, ext):
    return pl.pallas_call(
        kernel_a,
        out_shape=(shaped(96, 128), shaped(3, 14, 24, 256), shaped(3, 8, 8, 128), shaped(3, 22, 24, 256)),
        in_specs=[IN_SMEM, IN_VMEM],
        out_specs=(IN_VMEM,) * 4,
        scratch_shapes=[scratch(6, 22, 24, 256)] + [scratch(3, 22, 24, 256)] * 5,
        **PARAMS,
    )(moduli, ext)


def call_b(got):
    one, two = (3, 34, 16, 128), (3, 64, 128)
    return pl.pallas_call(
        kernel_b,
        out_shape=(shaped(2, 16, 128),) + (shaped(*one),) * 3 + (shaped(*two),) * 3,
        in_specs=[IN_VMEM],
        out_specs=(IN_VMEM,) * 7,
        scratch_shapes=[scratch(6, 34, 16, 128)] + [scratch(*one)] * 5,
        **PARAMS,
    )(got)


def call_c(place, got, level1, level2, level0):
    one, zero = (3, 34, 16, 128), (3, 22, 24, 256)
    return pl.pallas_call(
        kernel_c,
        out_shape=(shaped(3, 8, 8, 128), shaped(3, 8, 8, 128)),
        in_specs=[IN_SMEM] + [IN_VMEM] * 10,
        out_specs=(IN_VMEM,) * 2,
        scratch_shapes=[scratch(3, 16, 32, 128), scratch(272, 128), scratch(*one)]
        + [scratch(6, 34, 16, 128)] + [scratch(*one)] * 5
        + [scratch(6, 22, 24, 256)] + [scratch(*zero)] * 5,
        **PARAMS,
    )(place, got, *level1, *level2, *level0)


def both_ways(to_next, to_before, axis):
    count = lax.axis_size(axis)
    up = [(i, i + 1) for i in range(count - 1)]
    down = [(j, i) for i, j in up]
    return lax.ppermute(to_next, axis, up), lax.ppermute(to_before, axis, down)


def extend(body_forces, material, fixed_mask):
    cells = jnp.concatenate(
        [body_forces, (material + 1).astype(F32)[None], (1 - fixed_mask).astype(F32)[None]], axis=0
    )
    before, after = both_ways(cells, cells, "gz")
    halo = jnp.where(iota((1, 1, 1, 128), 3) < 64, after, before)
    cells = jnp.concatenate([cells, halo], axis=3)
    before, after = both_ways(cells[:, 1:8], cells[:, 0:7], "gx")
    cells = jnp.concatenate([before, cells, after], axis=1)
    before, after = both_ways(cells, cells, "gy")
    return jnp.concatenate([cells, after, before], axis=2)


def to_all(block, axes, count):
    copies = jnp.broadcast_to(block[None], (count,) + block.shape)
    return lax.all_to_all(copies, axes, 0, 0, tiled=True)


def body(body_forces, material, fixed_mask, moduli):
    ext = extend(body_forces, material, fixed_mask)
    send, r0, x0, mod0 = call_a(moduli, ext)
    send, mod1, x1, r1, mod2, x2, r2 = call_b(to_all(send, ("gx", "gy"), 32))
    got = to_all(send, "gz", 16)
    place = jnp.stack([lax.axis_index("gx"), lax.axis_index("gy"), lax.axis_index("gz")]).astype(jnp.int32)
    return call_c(place, got, (mod1, x1, r1), (mod2, x2, r2), (mod0, x0, r0))


def solution(mesh):
    cells = P(None, "gx", "gy", "gz")
    part = P("gx", "gy", "gz")
    return jax.shard_map(
        body, mesh=mesh, in_specs=(cells, part, part, P()), out_specs=(cells, cells), check_vma=False
    )
```

```python
import jax
import jax.numpy as jnp
from jax import lax
from jax.experimental import pallas as pl
from jax.experimental.pallas import tpu as pltpu
from jax.sharding import PartitionSpec as P

F32 = jnp.float32
CLASSES = 16
THETA = 1.125
HALF = 0.875
SIGMA = THETA / HALF
VMEM_LIMIT = 28 * 1024 * 1024


def cheb_factors():
    rho = 1.0 / SIGMA
    found = []
    for _ in range(2):
        rho_next = 1.0 / (2.0 * SIGMA - rho)
        found.append((rho_next * rho, 2.0 * rho_next / HALF))
        rho = rho_next
    return found


CHEB = cheb_factors()
START = (0.0, 1.0 / THETA)


BF16 = jnp.bfloat16


def split(v):
    high = v.astype(BF16)
    return high, (v - high.astype(F32)).astype(BF16)


def mxu(a, b, b_dim=0):
    return lax.dot_general(a, b, (((1,), (b_dim,)), ((), ())), preferred_element_type=F32)


def dot_l(picks, v):
    high, low = split(v)
    picks = picks.astype(BF16)
    return mxu(picks, high) + mxu(picks, low)


def dot_r(v, picks):
    high, low = split(v)
    picks = picks.astype(BF16)
    return mxu(high, picks) + mxu(low, picks)


def dot_l_nt(picks, v):
    high, low = split(v)
    picks = picks.astype(BF16)
    return mxu(picks, high, 1) + mxu(picks, low, 1)


def dot_r_nt(v, picks):
    high, low = split(v)
    picks = picks.astype(BF16)
    return mxu(high, picks, 1) + mxu(low, picks, 1)


def iota(shape, dim):
    return lax.broadcasted_iota(jnp.int32, shape, dim)


def ones_where(cond):
    return jnp.where(cond, 1.0, 0.0).astype(F32)


def roll(v, shift, axis):
    size = v.shape[axis]
    return pltpu.roll(v, shift % size, axis)


def loop(lo, hi, body):
    count = hi - lo
    step = max(k for k in (1, 2, 3, 4, 5) if count % k == 0)

    def several(n, carry):
        for k in range(step):
            body(lo + n * step + k)
        return carry

    lax.fori_loop(0, count // step, several, 0)


def neighbours_y(v, rows_masked):
    down, up = roll(v, 1, 0), roll(v, -1, 0)
    if rows_masked:
        row = iota(v.shape, 0)
        down = jnp.where(row >= 1, down, 0.0)
        up = jnp.where(row <= v.shape[0] - 2, up, 0.0)
    return down, up


def plane_factors(mod, scale, faces, diag, inv, lo, hi, rows_masked):
    half = 0.5 * scale

    def body(i):
        def fields(j):
            shear, lame = mod[0, j], mod[1, j]
            return half * shear, half * (shear + lame)

        p, g = fields(i)
        pm, gm = fields(i - 1)
        pp, gp = fields(i + 1)
        a, am = mod[2, i], mod[2, i - 1]
        pyd, pyu = neighbours_y(p, rows_masked)
        gyd, gyu = neighbours_y(g, rows_masked)
        ayd, _ = neighbours_y(a, rows_masked)
        pzd, pzu = roll(p, 1, 1), roll(p, -1, 1)
        gzd, gzu = roll(g, 1, 1), roll(g, -1, 1)
        azd = roll(a, 1, 1)
        base = (pm + pp) + (pyd + pyu) + (pzd + pzu) + 6.0 * p
        extra = (gm + gp, gyd + gyu, gzd + gzu)
        for c in range(3):
            d = a * (base + (extra[c] + 2.0 * g)) + (1.0 - a)
            diag[c, i] = d
            inv[c, i] = 1.0 / d
        for k, (pn, gn, an) in enumerate(((pm, gm, am), (pyd, gyd, ayd), (pzd, gzd, azd))):
            both = a * an
            face = p + pn
            faces[2 * k, i] = both * face
            faces[2 * k + 1, i] = both * (face + (g + gn))

    loop(lo, hi, body)


def plane_sweep(d, d_next, r_in, r_out, faces, diag, inv, lo, hi, pair, r_in_at=0, r_out_at=0):
    def body(i):
        for c in range(3):
            fx = faces[1 if c == 0 else 0, i]
            fxu = faces[1 if c == 0 else 0, i + 1]
            fy = faces[3 if c == 1 else 2, i]
            fz = faces[5 if c == 2 else 4, i]
            dc = d[c, i]
            t = fx * d[c, i - 1] + fxu * d[c, i + 1]
            t = t + (fy * roll(dc, 1, 0) + roll(fy * dc, -1, 0))
            t = t + (fz * roll(dc, 1, 1) + roll(fz * dc, -1, 1))
            r = r_in[c, i - r_in_at] - (diag[c, i] * dc - t)
            if r_out is not None:
                r_out[c, i - r_out_at] = r
            if pair is not None:
                new = (pair[1] * inv[c, i]) * r
                if pair[0] != 0.0:
                    new = new + pair[0] * dc
                d_next[c, i] = new

    loop(lo, hi, body)


def kernel_a(moduli, ext, send, r_out, x_out, mod, faces, diag, inv, d_a, d_b, r):
    def look_up(i):
        mat = ext[3, i]
        shear = jnp.zeros(mat.shape, F32)
        lame = jnp.zeros(mat.shape, F32)
        for k in range(CLASSES):
            hit = mat == float(k + 1)
            shear = jnp.where(hit, moduli[0, k], shear)
            lame = jnp.where(hit, moduli[1, k], lame)
        mod[0, i] = shear
        mod[1, i] = lame
        mod[2, i] = ext[4, i]

    loop(0, 22, look_up)
    plane_factors(mod, 1.0, faces, diag, inv, 1, 21, False)

    def start(i):
        for c in range(3):
            d_a[c, i] = (START[1] * inv[c, i]) * ext[c, i]

    loop(1, 21, start)
    plane_sweep(d_a, d_b, ext, r, faces, diag, inv, 2, 20, CHEB[0])
    for c in range(3):
        x_out[c] = d_a[c, 7:15, 0:8, 0:128] + d_b[c, 7:15, 0:8, 0:128]
    plane_sweep(d_b, d_a, r, r, faces, diag, inv, 3, 19, CHEB[1])
    for c in range(3):
        x_out[c] = x_out[c] + d_a[c, 7:15, 0:8, 0:128]
    plane_sweep(d_a, None, r, r_out, faces, diag, inv, 4, 18, None, 0, 4)
    rows = []
    for c in range(3):
        for j in range(4):
            rows.append(r_out[c, 3 + 2 * j, 0:8] + r_out[c, 4 + 2 * j, 0:8])
    for k in range(3):
        for j in range(4):
            rows.append(mod[k, 7 + 2 * j, 0:8] + mod[k, 8 + 2 * j, 0:8])
    stacked = jnp.concatenate(rows, axis=0)
    pair_z = ones_where(iota((256, 128), 0) // 2 == iota((256, 128), 1))
    pair_y = ones_where(iota((96, 192), 1) // 2 == iota((96, 192), 0))
    low = dot_l(pair_y, dot_r(stacked, pair_z))
    row = iota((96, 128), 0)
    low = jnp.where(row < 48, low, jnp.where(row < 80, 0.125 * low, ones_where(low > 0.5)))
    lane = iota((48, 128), 1)
    send[0:48] = jnp.where(lane < 64, low[0:48], roll(low[48:96], 64, 1))
    lane = iota((32, 128), 1)
    packed = jnp.zeros((32, 128), F32)
    for k in range(3):
        part = low[32 * k : 32 * k + 32]
        packed = jnp.where((lane >= 40 * k) & (lane < 40 * k + 20), roll(part, 40 * k - 64, 1), packed)
        packed = jnp.where((lane >= 40 * k + 20) & (lane < 40 * k + 40), roll(part, 40 * k - 88, 1), packed)
    send[48:80] = packed


def flat_factors(mods, steps, scales, groups):
    shear, lame, a = mods
    total = 0.0
    faces = []
    for (axis, shift, below, above), scale, share in zip(steps, scales, groups):
        h = (0.5 * scale) * (shear + share * (shear + lame))
        dn, up = roll(h, shift, axis), roll(h, -shift, axis)
        an = roll(a, shift, axis)
        if below is not None:
            dn = jnp.where(below, dn, 0.0)
            up = jnp.where(above, up, 0.0)
            an = jnp.where(below, an, 0.0)
        total = total + (2.0 * h + (dn + up))
        faces.append((a * an) * (h + dn))
    diag = a * total + (1.0 - a)
    return faces, diag, 1.0 / diag


def flat_apply(v, factors, steps):
    faces, diag, inv = factors
    out = diag * v
    for face, (axis, shift, below, above) in zip(faces, steps):
        out = out - (face * roll(v, shift, axis) + roll(face * v, -shift, axis))
    return out


def flat_smooth(x, r, factors, steps, last):
    inv = factors[2]
    d = (START[1] * inv) * r
    for sweep in range(3):
        x = d if x is None else x + d
        if sweep == 2 and not last:
            return x, None
        r = r - flat_apply(d, factors, steps)
        if sweep < 2:
            c1, c2 = CHEB[sweep]
            d = c1 * d + (c2 * inv) * r
    return x, r


def level2_steps():
    lane = iota((64, 128), 1)
    return (
        (1, 8, lane >= 8, lane < 120),
        (1, 1, lane % 8 >= 1, lane % 8 <= 6),
        (0, 1, None, None),
    )


def level3_steps(rows):
    lane = iota((rows, 128), 1)
    row = iota((rows, 128), 0)
    return (
        (1, 4, lane % 32 >= 4, lane % 32 < 28),
        (1, 1, lane % 4 >= 1, lane % 4 <= 2),
        (0, 1, row >= 1, row <= rows - 2),
    )


def level3_groups(rows):
    group = iota((rows, 128), 1) // 32
    return tuple(ones_where(group == k) for k in range(3))


def to_level3(k):
    cell = iota((128, 128), 0)
    lane = iota((128, 128), 1)
    return ones_where(lane == 32 * k + (cell // 16) * 4 + (cell % 8) // 2)


def kernel_b(got, send, mod1, x1, r1, mod2, x2, r2, faces, diag, inv, d_a, d_b, b1):
    sub = iota((8, 128), 0) < 4
    zero = jnp.zeros((16, 128), F32)
    for k in range(3):
        mod1[k, 0] = zero
        mod1[k, 33] = zero
        d_a[k, 0] = zero
        d_a[k, 33] = zero
        d_b[k, 0] = zero
        d_b[k, 33] = zero
    for k in range(6):
        faces[k, 33] = zero

    lane = iota((8, 128), 1)

    def tile(dev, t):
        own = got[dev, 8 * (t % 6) : 8 * (t % 6) + 8]
        if t >= 6:
            own = roll(own, 64, 1)
        halo = got[dev, 48 + 8 * (t % 4) : 56 + 8 * (t % 4)]
        after = roll(halo, 64 - 40 * (t // 4), 1)
        before = roll(halo, 88 - 40 * (t // 4), 1)
        halo = jnp.where(lane < 84, after, jnp.where(lane >= 108, before, 0.0))
        return jnp.where(lane < 64, own, halo)

    def unpack(gx, carry):
        for f in range(6):
            for pair in range(2):
                at = f * 2 + pair
                for half in range(2):
                    s0 = tile(gx * 4 + 2 * half, at)
                    s1 = tile(gx * 4 + 2 * half + 1, at)
                    even = jnp.where(sub, s0, roll(s1, 4, 0))
                    odd = jnp.where(sub, roll(s0, 4, 0), s1)
                    x = gx * 4 + 2 * pair + 1
                    rows = slice(8 * half, 8 * half + 8)
                    if f < 3:
                        b1[f, x, rows] = even
                        b1[f, x + 1, rows] = odd
                    else:
                        mod1[f - 3, x, rows] = even
                        mod1[f - 3, x + 1, rows] = odd
        return carry

    lax.fori_loop(0, 8, unpack, 0)
    plane_factors(mod1, 2.0, faces, diag, inv, 1, 33, True)

    def start(i):
        for c in range(3):
            d_a[c, i] = (START[1] * inv[c, i]) * b1[c, i]

    loop(1, 33, start)
    plane_sweep(d_a, d_b, b1, r1, faces, diag, inv, 1, 33, CHEB[0])
    for c in range(3):
        x1[c] = d_a[c] + d_b[c]
    plane_sweep(d_b, d_a, r1, r1, faces, diag, inv, 1, 33, CHEB[1])
    for c in range(3):
        x1[c] = x1[c] + d_a[c]
    plane_sweep(d_a, None, r1, r1, faces, diag, inv, 1, 33, None)

    pair_y = ones_where(iota((128, 256), 1) // 2 == iota((128, 256), 0))
    pair_z = ones_where(iota((64, 128), 1) // 2 == iota((64, 128), 0))

    def restrict(ref, k):
        planes = [ref[k, 1 + 2 * j] + ref[k, 2 + 2 * j] for j in range(16)]
        return dot_l_nt(pair_z, dot_l(pair_y, jnp.concatenate(planes, axis=0)))

    shear = 0.125 * restrict(mod1, 0)
    lame = 0.125 * restrict(mod1, 1)
    active = ones_where(restrict(mod1, 2) > 0.5)
    mod2[0] = shear
    mod2[1] = lame
    mod2[2] = active
    steps = level2_steps()
    own_z = ones_where(iota((16, 64), 1) // 2 == iota((16, 64), 0))
    low = jnp.zeros((16, 128), F32)
    for c in range(3):
        shares = tuple(1.0 if c == k else 0.0 for k in range(3))
        factors = flat_factors((shear, lame, active), steps, (4.0, 4.0, 4.0), shares)
        x, r = flat_smooth(None, restrict(r1, c), factors, steps, True)
        x2[c] = x
        r2[c] = r
        low = low + dot_r(dot_l(own_z, r), to_level3(c))
    send[0] = low
    lane = iota((16, 128), 1)
    low = dot_r(dot_l(own_z, shear), to_level3(0)) + dot_r(dot_l(own_z, lame), to_level3(1))
    low = 0.125 * low
    low = low + ones_where(dot_r(dot_l(own_z, active), to_level3(2)) > 0.5)
    send[1] = low


def spread(v, group):
    lane = iota(v.shape, 1)
    v = jnp.where(lane // 32 == group, v, 0.0)
    back = roll(v, -32 * group, 1)
    return back + roll(back, 32, 1) + roll(back, 64, 1)


def eliminate(mat, cells):
    tiles = [jnp.stack([mat[c, k, 8 * t : 8 * t + 8] for c, k in cells]) for t in range(4)]
    rows = iota(tiles[0].shape, 1)
    for p in range(0, 32, 2):
        at, q = divmod(p, 8)
        row0, row1 = tiles[at][:, q : q + 1, :], tiles[at][:, q + 1 : q + 2, :]
        a00, a01 = row0[:, :, p : p + 1], row0[:, :, p + 1 : p + 2]
        a10, a11 = row1[:, :, p : p + 1], row1[:, :, p + 1 : p + 2]
        scale = 1.0 / (a00 * a11 - a01 * a10)
        new0 = (a11 * scale) * row0 - (a01 * scale) * row1
        new1 = (a00 * scale) * row1 - (a10 * scale) * row0
        for t in range(4):
            a = tiles[t]
            a = a - (a[:, :, p : p + 1] * new0 + a[:, :, p + 1 : p + 2] * new1)
            if t == at:
                a = jnp.where(rows == q, new0, jnp.where(rows == q + 1, new1, a))
            tiles[t] = a
    for n, (c, k) in enumerate(cells):
        for t in range(4):
            mat[c, k, 8 * t : 8 * t + 8] = tiles[t][n]


def coarse_solve(mods3, rest, mat):
    blocks = ones_where(iota((16, 256), 1) // 16 == iota((16, 256), 0))
    shear = 0.0625 * dot_l(blocks, mods3[0])
    lame = 0.0625 * dot_l(blocks, mods3[1])
    active = ones_where(dot_l(blocks, mods3[2]) > 0.5)
    side = dot_l(blocks, rest)
    steps = level3_steps(16)
    scales = (128.0, 128.0, 0.5)
    faces, diag, _ = flat_factors((shear, lame, active), steps, scales, level3_groups(16))
    uppers = []
    for face, (axis, shift, below, above) in zip(faces, steps):
        uppers.append(jnp.where(above, roll(face, -shift, axis), 0.0))
    lane16 = iota((16, 128), 1)
    row = iota((32, 128), 0)
    lane = iota((32, 128), 1)
    at_diag = lane % 32 == row
    inner = lane < 32
    patterns = (inner & (lane == row - 4), inner & (lane == row + 4), inner & (lane == row - 1), inner & (lane == row + 1))
    columns = jnp.concatenate([faces[2], uppers[2]] + [jnp.zeros((16, 128), F32)] * 6, axis=0).T
    for c in range(3):
        first = jnp.where(
            lane16 < 32,
            roll(diag, -32 * c, 1),
            jnp.where(
                lane16 < 64,
                -roll(faces[2], 32 - 32 * c, 1),
                jnp.where(lane16 < 96, -roll(uppers[2], 64 - 32 * c, 1), roll(side, 96 - 32 * c, 1)),
            ),
        )
        others = [-roll(v, -32 * c, 1) for v in (uppers[0], faces[0], uppers[1], faces[1])]
        for k in range(16):
            m = jnp.where(at_diag, first[k : k + 1], 0.0)
            for pattern, v in zip(patterns, others):
                m = jnp.where(pattern, v[k : k + 1], m)
            mat[c, k] = m

    lane_t = inner
    lane_l = (lane >= 32) & (lane < 64)
    lane_r = (lane >= 64) & (lane < 96)
    lane_b = lane >= 96
    keep = lane_t | lane_b
    none = jnp.zeros((32, 128), F32)
    for h in (1, 2, 4, 8):
        eliminate(mat, [(c, k) for c in range(3) for k in range(h, 16, 2 * h)])
        for c in range(3):
            for k in range(0, 16, 2 * h):
                m = mat[c, k]
                left, right = none, none
                if k - h >= 0:
                    w = mat[c, k - h]
                    left = jnp.where(lane_t, roll(w, 64, 1), jnp.where(lane_l | lane_b, w, 0.0))
                if k + h < 16:
                    w = mat[c, k + h]
                    right = jnp.where(lane_t, roll(w, 96, 1), jnp.where(lane_r | lane_b, w, 0.0))
                if h == 1:
                    part = columns[32 * c : 32 * c + 32]
                    change = -(part[:, k : k + 1] * left + part[:, 16 + k : 17 + k] * right)
                else:
                    high, low = split(roll(m, -32, 1))
                    both = jnp.where(lane < 64, high.astype(F32), roll(low.astype(F32), 64, 1)).astype(BF16)
                    w_high, w_low = split(jnp.concatenate([left, right], axis=0))
                    change = mxu(
                        jnp.concatenate([both, both], axis=1),
                        jnp.concatenate([w_high, w_high, w_low, w_low], axis=0),
                    )
                mat[c, k] = jnp.where(keep, m, 0.0) - change
    eliminate(mat, [(c, 0) for c in range(3)])
    pieces = []
    found = {}
    for c in range(3):
        found[c, 0] = jnp.sum(jnp.where(lane_b, mat[c, 0], 0.0), axis=1, keepdims=True)
    for h in (8, 4, 2, 1):
        for c in range(3):
            for k in range(h, 16, 2 * h):
                v = jnp.where(lane_l & at_diag, -found[c, k - h], 0.0)
                if k + h < 16:
                    v = jnp.where(lane_r & at_diag, -found[c, k + h], v)
                v = jnp.sum(v, axis=0, keepdims=True)
                v = jnp.where(lane_b[0:1], 1.0, v)
                found[c, k] = jnp.sum(mat[c, k] * v, axis=1, keepdims=True)
    for c in range(3):
        piece = none
        for k in range(16):
            piece = jnp.where(lane == k, found[c, k], piece)
        pieces.append(piece)
    pieces.append(none)
    whole = jnp.concatenate(pieces, axis=0)
    again = ones_where(iota((256, 128), 0) // 16 == iota((256, 128), 1))
    return dot_l_nt(again, whole)


def kernel_c(
    place, got, mod1, x1, r1, mod2, x2, r2, mod0, x0, r0, disp, resid,
    mat, e3, e1, faces1, diag1, inv1, d1a, d1b, r1w, faces, diag, inv, d_a, d_b, r_w,
):
    gx, gy, gz = place[0], place[1], place[2]
    b3 = jnp.concatenate([got[k, 0] for k in range(16)], axis=0)
    m3 = jnp.concatenate([got[k, 1] for k in range(16)], axis=0)
    mods3 = tuple(spread(m3, k) for k in range(3))
    steps = level3_steps(256)
    factors = flat_factors(mods3, steps, (8.0, 8.0, 8.0), level3_groups(256))
    x, r = flat_smooth(None, b3, factors, steps, True)
    corr = coarse_solve(mods3, r, mat)
    x = x + corr
    r = r - flat_apply(corr, factors, steps)
    x, _ = flat_smooth(x, r, factors, steps, False)
    e3[0:8] = jnp.zeros((8, 128), F32)
    e3[264:272] = jnp.zeros((8, 128), F32)
    e3[8:264] = x
    base = pl.multiple_of(gz * 16, 16)
    own = e3[pl.ds(base + 8, 24)]
    before = e3[pl.ds(base, 8)]
    slab = jnp.concatenate([own, before], axis=0)
    slab = dot_l(ones_where(iota((64, 32), 0) // 2 == iota((64, 32), 1)), slab)
    steps = level2_steps()
    mods = (mod2[0], mod2[1], mod2[2])
    for k in range(3):
        e1[k, 0] = jnp.zeros((16, 128), F32)
        e1[k, 33] = jnp.zeros((16, 128), F32)
        d1a[k, 0] = jnp.zeros((16, 128), F32)
        d1a[k, 33] = jnp.zeros((16, 128), F32)
        d1b[k, 0] = jnp.zeros((16, 128), F32)
        d1b[k, 33] = jnp.zeros((16, 128), F32)
    for k in range(6):
        faces1[k, 33] = jnp.zeros((16, 128), F32)
    up_xy = ones_where(
        ((iota((512, 128), 0) // 32) * 8 + (iota((512, 128), 0) % 16) // 2) == iota((512, 128), 1)
    )
    up_z = ones_where(iota((64, 128), 1) // 2 == iota((64, 128), 0))
    for c in range(3):
        shares = tuple(1.0 if c == k else 0.0 for k in range(3))
        factors = flat_factors(mods, steps, (4.0, 4.0, 4.0), shares)
        corr = dot_r_nt(slab, to_level3(c))
        x = x2[c] + corr
        r = r2[c] - flat_apply(corr, factors, steps)
        x, _ = flat_smooth(x, r, factors, steps, False)
        lifted = dot_l(up_xy, dot_r(x.T, up_z))
        for j in range(32):
            e1[c, j + 1] = lifted[16 * j : 16 * j + 16]
    plane_factors(mod1, 2.0, faces1, diag1, inv1, 1, 33, True)
    plane_sweep(e1, d1a, r1, r1w, faces1, diag1, inv1, 1, 33, START)
    for c in range(3):
        e1[c, 1:33] = e1[c, 1:33] + x1[c, 1:33] + d1a[c, 1:33]
    plane_sweep(d1a, d1b, r1w, r1w, faces1, diag1, inv1, 1, 33, CHEB[0])
    for c in range(3):
        e1[c, 1:33] = e1[c, 1:33] + d1b[c, 1:33]
    plane_sweep(d1b, d1a, r1w, None, faces1, diag1, inv1, 1, 33, CHEB[1])
    for c in range(3):
        e1[c, 1:33] = e1[c, 1:33] + d1a[c, 1:33]
    row = iota((24, 16), 0)
    row = jnp.where(row >= 16, row - 24, row)
    up_y = ones_where((row + 8 * gy + 16) // 2 - 8 == iota((24, 16), 1))
    up_z0 = ones_where(iota((128, 256), 1) // 2 == iota((128, 256), 0))
    planes = []
    for c in range(3):
        for j in range(8):
            planes.append(e1[c, jnp.clip(4 * gx + (j - 1), 0, 33)])
    lifted = dot_r(jnp.concatenate(planes, axis=0), up_z0)
    up_y = jnp.concatenate([up_y, up_y], axis=1).astype(BF16)
    for c in range(3):
        for j in range(8):
            at = 16 * (8 * c + j)
            high, low = split(lifted[at : at + 16])
            plane = mxu(up_y, jnp.concatenate([high, low], axis=0))
            d_b[c, 3 + 2 * j] = plane
            d_b[c, 4 + 2 * j] = plane
    plane_factors(mod0, 1.0, faces, diag, inv, 4, 19, False)
    own_part = (slice(7, 15), slice(0, 8), slice(0, 128))
    for c in range(3):
        disp[c] = x0[c] + d_b[(c,) + own_part]
    plane_sweep(d_b, d_a, r0, r_w, faces, diag, inv, 4, 18, START, 4, 0)
    for c in range(3):
        disp[c] = disp[c] + d_a[(c,) + own_part]
    plane_sweep(d_a, d_b, r_w, r_w, faces, diag, inv, 5, 17, CHEB[0])
    for c in range(3):
        disp[c] = disp[c] + d_b[(c,) + own_part]
    plane_sweep(d_b, d_a, r_w, r_w, faces, diag, inv, 6, 16, CHEB[1])
    for c in range(3):
        disp[c] = disp[c] + d_a[(c,) + own_part]
    plane_sweep(d_a, None, r_w, r_w, faces, diag, inv, 7, 15, None)
    for c in range(3):
        resid[c] = r_w[(c,) + own_part]


IN_VMEM = pl.BlockSpec(memory_space=pltpu.VMEM)
IN_SMEM = pl.BlockSpec(memory_space=pltpu.SMEM)


def shaped(*shape):
    return jax.ShapeDtypeStruct(shape, F32)


def scratch(*shape):
    return pltpu.VMEM(shape, F32)


PARAMS = dict(compiler_params=pltpu.CompilerParams(vmem_limit_bytes=VMEM_LIMIT))


def call_a(moduli, ext):
    return pl.pallas_call(
        kernel_a,
        out_shape=(shaped(80, 128), shaped(3, 14, 24, 256), shaped(3, 8, 8, 128), shaped(3, 22, 24, 256)),
        in_specs=[IN_SMEM, IN_VMEM],
        out_specs=(IN_VMEM,) * 4,
        scratch_shapes=[scratch(6, 22, 24, 256)] + [scratch(3, 22, 24, 256)] * 5,
        **PARAMS,
    )(moduli, ext)


def call_b(got):
    one, two = (3, 34, 16, 128), (3, 64, 128)
    return pl.pallas_call(
        kernel_b,
        out_shape=(shaped(2, 16, 128),) + (shaped(*one),) * 3 + (shaped(*two),) * 3,
        in_specs=[IN_VMEM],
        out_specs=(IN_VMEM,) * 7,
        scratch_shapes=[scratch(6, 34, 16, 128)] + [scratch(*one)] * 5,
        **PARAMS,
    )(got)


def call_c(place, got, level1, level2, level0):
    one, zero = (3, 34, 16, 128), (3, 22, 24, 256)
    return pl.pallas_call(
        kernel_c,
        out_shape=(shaped(3, 8, 8, 128), shaped(3, 8, 8, 128)),
        in_specs=[IN_SMEM] + [IN_VMEM] * 10,
        out_specs=(IN_VMEM,) * 2,
        scratch_shapes=[scratch(3, 16, 32, 128), scratch(272, 128), scratch(*one)]
        + [scratch(6, 34, 16, 128)] + [scratch(*one)] * 5
        + [scratch(6, 22, 24, 256)] + [scratch(*zero)] * 5,
        **PARAMS,
    )(place, got, *level1, *level2, *level0)


def both_ways(to_next, to_before, axis):
    count = lax.axis_size(axis)
    up = [(i, i + 1) for i in range(count - 1)]
    down = [(j, i) for i, j in up]
    return lax.ppermute(to_next, axis, up), lax.ppermute(to_before, axis, down)


def extend(body_forces, material, fixed_mask):
    cells = jnp.concatenate(
        [body_forces, (material + 1).astype(F32)[None], (1 - fixed_mask).astype(F32)[None]], axis=0
    )
    before, after = both_ways(cells, cells, "gz")
    halo = jnp.where(iota((1, 1, 1, 128), 3) < 64, after, before)
    cells = jnp.concatenate([cells, halo], axis=3)
    before, after = both_ways(cells[:, 1:8], cells[:, 0:7], "gx")
    cells = jnp.concatenate([before, cells, after], axis=1)
    before, after = both_ways(cells, cells, "gy")
    return jnp.concatenate([cells, after, before], axis=2)


def to_all(block, axes, count):
    copies = jnp.broadcast_to(block[None], (count,) + block.shape)
    return lax.all_to_all(copies, axes, 0, 0, tiled=True)


def body(body_forces, material, fixed_mask, moduli):
    ext = extend(body_forces, material, fixed_mask)
    send, r0, x0, mod0 = call_a(moduli, ext)
    send, mod1, x1, r1, mod2, x2, r2 = call_b(to_all(send, ("gx", "gy"), 32))
    got = to_all(send, "gz", 16)
    place = jnp.stack([lax.axis_index("gx"), lax.axis_index("gy"), lax.axis_index("gz")]).astype(jnp.int32)
    return call_c(place, got, (mod1, x1, r1), (mod2, x2, r2), (mod0, x0, r0))


def solution(mesh):
    cells = P(None, "gx", "gy", "gz")
    part = P("gx", "gy", "gz")
    return jax.shard_map(
        body, mesh=mesh, in_specs=(cells, part, part, P()), out_specs=(cells, cells), check_vma=False
    )
```

```python
import jax
import jax.numpy as jnp
from jax import lax
from jax.experimental import pallas as pl
from jax.experimental.pallas import tpu as pltpu
from jax.sharding import PartitionSpec as P

F32 = jnp.float32
CLASSES = 16
THETA = 1.125
HALF = 0.875
SIGMA = THETA / HALF
VMEM_LIMIT = 36 * 1024 * 1024


def cheb_factors():
    rho = 1.0 / SIGMA
    found = []
    for _ in range(2):
        rho_next = 1.0 / (2.0 * SIGMA - rho)
        found.append((rho_next * rho, 2.0 * rho_next / HALF))
        rho = rho_next
    return found


CHEB = cheb_factors()
START = (0.0, 1.0 / THETA)


BF16 = jnp.bfloat16


def split(v):
    high = v.astype(BF16)
    return high, (v - high.astype(F32)).astype(BF16)


def mxu(a, b, b_dim=0):
    return lax.dot_general(a, b, (((1,), (b_dim,)), ((), ())), preferred_element_type=F32)


def dot_l(picks, v):
    high, low = split(v)
    picks = picks.astype(BF16)
    return mxu(picks, high) + mxu(picks, low)


def dot_r(v, picks):
    high, low = split(v)
    picks = picks.astype(BF16)
    return mxu(high, picks) + mxu(low, picks)


def dot_l_nt(picks, v):
    high, low = split(v)
    picks = picks.astype(BF16)
    return mxu(picks, high, 1) + mxu(picks, low, 1)


def dot_r_nt(v, picks):
    high, low = split(v)
    picks = picks.astype(BF16)
    return mxu(high, picks, 1) + mxu(low, picks, 1)


def iota(shape, dim):
    return lax.broadcasted_iota(jnp.int32, shape, dim)


def ones_where(cond):
    return jnp.where(cond, 1.0, 0.0).astype(F32)


def roll(v, shift, axis):
    size = v.shape[axis]
    return pltpu.roll(v, shift % size, axis)


def loop(lo, hi, body):
    count = hi - lo
    step = max(k for k in (1, 2, 3, 4, 5) if count % k == 0)

    def several(n, carry):
        for k in range(step):
            body(lo + n * step + k)
        return carry

    lax.fori_loop(0, count // step, several, 0)


def neighbours_y(v, rows_masked):
    down, up = roll(v, 1, 0), roll(v, -1, 0)
    if rows_masked:
        row = iota(v.shape, 0)
        down = jnp.where(row >= 1, down, 0.0)
        up = jnp.where(row <= v.shape[0] - 2, up, 0.0)
    return down, up


def plane_factors(mod, scale, faces, diag, inv, lo, hi, rows_masked):
    half = 0.5 * scale

    def body(i):
        def fields(j):
            shear, lame = mod[0, j], mod[1, j]
            return half * shear, half * (shear + lame)

        p, g = fields(i)
        pm, gm = fields(i - 1)
        pp, gp = fields(i + 1)
        a, am = mod[2, i], mod[2, i - 1]
        pyd, pyu = neighbours_y(p, rows_masked)
        gyd, gyu = neighbours_y(g, rows_masked)
        ayd, _ = neighbours_y(a, rows_masked)
        pzd, pzu = roll(p, 1, 1), roll(p, -1, 1)
        gzd, gzu = roll(g, 1, 1), roll(g, -1, 1)
        azd = roll(a, 1, 1)
        base = (pm + pp) + (pyd + pyu) + (pzd + pzu) + 6.0 * p
        extra = (gm + gp, gyd + gyu, gzd + gzu)
        for c in range(3):
            d = a * (base + (extra[c] + 2.0 * g)) + (1.0 - a)
            diag[c, i] = d
            inv[c, i] = 1.0 / d
        for k, (pn, gn, an) in enumerate(((pm, gm, am), (pyd, gyd, ayd), (pzd, gzd, azd))):
            both = a * an
            face = p + pn
            faces[2 * k, i] = both * face
            faces[2 * k + 1, i] = both * (face + (g + gn))

    loop(lo, hi, body)


def plane_sweep(d, d_next, r_in, r_out, faces, diag, inv, lo, hi, pair, r_in_at=0, r_out_at=0):
    def body(i):
        for c in range(3):
            fx = faces[1 if c == 0 else 0, i]
            fxu = faces[1 if c == 0 else 0, i + 1]
            fy = faces[3 if c == 1 else 2, i]
            fz = faces[5 if c == 2 else 4, i]
            dc = d[c, i]
            t = fx * d[c, i - 1] + fxu * d[c, i + 1]
            t = t + (fy * roll(dc, 1, 0) + roll(fy * dc, -1, 0))
            t = t + (fz * roll(dc, 1, 1) + roll(fz * dc, -1, 1))
            r = r_in[c, i - r_in_at] - (diag[c, i] * dc - t)
            if r_out is not None:
                r_out[c, i - r_out_at] = r
            if pair is not None:
                new = (pair[1] * inv[c, i]) * r
                if pair[0] != 0.0:
                    new = new + pair[0] * dc
                d_next[c, i] = new

    loop(lo, hi, body)


def kernel_a(moduli, ext, send, r_out, x_out, mod, faces, diag, inv, d_a, d_b, r):
    def look_up(i):
        mat = ext[3, i]
        shear = jnp.zeros(mat.shape, F32)
        lame = jnp.zeros(mat.shape, F32)
        for k in range(CLASSES):
            hit = mat == float(k + 1)
            shear = jnp.where(hit, moduli[0, k], shear)
            lame = jnp.where(hit, moduli[1, k], lame)
        mod[0, i] = shear
        mod[1, i] = lame
        mod[2, i] = ext[4, i]

    loop(0, 22, look_up)
    plane_factors(mod, 1.0, faces, diag, inv, 1, 21, False)

    def start(i):
        for c in range(3):
            d_a[c, i] = (START[1] * inv[c, i]) * ext[c, i]

    loop(1, 21, start)
    plane_sweep(d_a, d_b, ext, r, faces, diag, inv, 2, 20, CHEB[0])
    for c in range(3):
        x_out[c] = d_a[c, 7:15, 0:8, 0:128] + d_b[c, 7:15, 0:8, 0:128]
    plane_sweep(d_b, d_a, r, r, faces, diag, inv, 3, 19, CHEB[1])
    for c in range(3):
        x_out[c] = x_out[c] + d_a[c, 7:15, 0:8, 0:128]
    plane_sweep(d_a, None, r, r_out, faces, diag, inv, 4, 18, None, 0, 4)
    rows = []
    for c in range(3):
        for j in range(4):
            rows.append(r_out[c, 3 + 2 * j, 0:8] + r_out[c, 4 + 2 * j, 0:8])
    for k in range(3):
        for j in range(4):
            rows.append(mod[k, 7 + 2 * j, 0:8] + mod[k, 8 + 2 * j, 0:8])
    stacked = jnp.concatenate(rows, axis=0)
    pair_z = ones_where(iota((256, 128), 0) // 2 == iota((256, 128), 1))
    pair_y = ones_where(iota((96, 192), 1) // 2 == iota((96, 192), 0))
    low = dot_l(pair_y, dot_r(stacked, pair_z))
    row = iota((96, 128), 0)
    low = jnp.where(row < 48, low, jnp.where(row < 80, 0.125 * low, ones_where(low > 0.5)))
    lane = iota((48, 128), 1)
    send[0:48] = jnp.where(lane < 64, low[0:48], roll(low[48:96], 64, 1))
    lane = iota((32, 128), 1)
    packed = jnp.zeros((32, 128), F32)
    for k in range(3):
        part = low[32 * k : 32 * k + 32]
        packed = jnp.where((lane >= 40 * k) & (lane < 40 * k + 20), roll(part, 40 * k - 64, 1), packed)
        packed = jnp.where((lane >= 40 * k + 20) & (lane < 40 * k + 40), roll(part, 40 * k - 88, 1), packed)
    send[48:80] = packed


def flat_factors(mods, steps, scales, groups):
    shear, lame, a = mods
    total = 0.0
    faces = []
    for (axis, shift, below, above), scale, share in zip(steps, scales, groups):
        h = (0.5 * scale) * (shear + share * (shear + lame))
        dn, up = roll(h, shift, axis), roll(h, -shift, axis)
        an = roll(a, shift, axis)
        if below is not None:
            dn = jnp.where(below, dn, 0.0)
            up = jnp.where(above, up, 0.0)
            an = jnp.where(below, an, 0.0)
        total = total + (2.0 * h + (dn + up))
        faces.append((a * an) * (h + dn))
    diag = a * total + (1.0 - a)
    return faces, diag, 1.0 / diag


def flat_apply(v, factors, steps):
    faces, diag, inv = factors
    out = diag * v
    for face, (axis, shift, below, above) in zip(faces, steps):
        out = out - (face * roll(v, shift, axis) + roll(face * v, -shift, axis))
    return out


def flat_smooth(x, r, factors, steps, last):
    inv = factors[2]
    d = (START[1] * inv) * r
    for sweep in range(3):
        x = d if x is None else x + d
        if sweep == 2 and not last:
            return x, None
        r = r - flat_apply(d, factors, steps)
        if sweep < 2:
            c1, c2 = CHEB[sweep]
            d = c1 * d + (c2 * inv) * r
    return x, r


def level2_steps():
    lane = iota((64, 128), 1)
    return (
        (1, 8, lane >= 8, lane < 120),
        (1, 1, lane % 8 >= 1, lane % 8 <= 6),
        (0, 1, None, None),
    )


def level3_steps(rows):
    lane = iota((rows, 128), 1)
    row = iota((rows, 128), 0)
    return (
        (1, 4, lane % 32 >= 4, lane % 32 < 28),
        (1, 1, lane % 4 >= 1, lane % 4 <= 2),
        (0, 1, row >= 1, row <= rows - 2),
    )


def level3_groups(rows):
    group = iota((rows, 128), 1) // 32
    return tuple(ones_where(group == k) for k in range(3))


def to_level3(k):
    cell = iota((128, 128), 0)
    lane = iota((128, 128), 1)
    return ones_where(lane == 32 * k + (cell // 16) * 4 + (cell % 8) // 2)


def kernel_b(got, send, mod1, x1, r1, mod2, x2, r2, faces, diag, inv, d_a, d_b, b1):
    sub = iota((8, 128), 0) < 4
    zero = jnp.zeros((16, 128), F32)
    for k in range(3):
        mod1[k, 0] = zero
        mod1[k, 33] = zero
        d_a[k, 0] = zero
        d_a[k, 33] = zero
        d_b[k, 0] = zero
        d_b[k, 33] = zero
    for k in range(6):
        faces[k, 33] = zero

    lane = iota((8, 128), 1)

    def tile(dev, t):
        own = got[dev, 8 * (t % 6) : 8 * (t % 6) + 8]
        if t >= 6:
            own = roll(own, 64, 1)
        halo = got[dev, 48 + 8 * (t % 4) : 56 + 8 * (t % 4)]
        after = roll(halo, 64 - 40 * (t // 4), 1)
        before = roll(halo, 88 - 40 * (t // 4), 1)
        halo = jnp.where(lane < 84, after, jnp.where(lane >= 108, before, 0.0))
        return jnp.where(lane < 64, own, halo)

    def unpack(gx, carry):
        for f in range(6):
            for pair in range(2):
                at = f * 2 + pair
                for half in range(2):
                    s0 = tile(gx * 4 + 2 * half, at)
                    s1 = tile(gx * 4 + 2 * half + 1, at)
                    even = jnp.where(sub, s0, roll(s1, 4, 0))
                    odd = jnp.where(sub, roll(s0, 4, 0), s1)
                    x = gx * 4 + 2 * pair + 1
                    rows = slice(8 * half, 8 * half + 8)
                    if f < 3:
                        b1[f, x, rows] = even
                        b1[f, x + 1, rows] = odd
                    else:
                        mod1[f - 3, x, rows] = even
                        mod1[f - 3, x + 1, rows] = odd
        return carry

    lax.fori_loop(0, 8, unpack, 0)
    plane_factors(mod1, 2.0, faces, diag, inv, 1, 33, True)

    def start(i):
        for c in range(3):
            d_a[c, i] = (START[1] * inv[c, i]) * b1[c, i]

    loop(1, 33, start)
    plane_sweep(d_a, d_b, b1, r1, faces, diag, inv, 1, 33, CHEB[0])
    for c in range(3):
        x1[c] = d_a[c] + d_b[c]
    plane_sweep(d_b, d_a, r1, r1, faces, diag, inv, 1, 33, CHEB[1])
    for c in range(3):
        x1[c] = x1[c] + d_a[c]
    plane_sweep(d_a, None, r1, r1, faces, diag, inv, 1, 33, None)

    pair_y = ones_where(iota((128, 256), 1) // 2 == iota((128, 256), 0))
    pair_z = ones_where(iota((64, 128), 1) // 2 == iota((64, 128), 0))

    def restrict(ref, k):
        planes = [ref[k, 1 + 2 * j] + ref[k, 2 + 2 * j] for j in range(16)]
        return dot_l_nt(pair_z, dot_l(pair_y, jnp.concatenate(planes, axis=0)))

    shear = 0.125 * restrict(mod1, 0)
    lame = 0.125 * restrict(mod1, 1)
    active = ones_where(restrict(mod1, 2) > 0.5)
    mod2[0] = shear
    mod2[1] = lame
    mod2[2] = active
    steps = level2_steps()
    own_z = ones_where(iota((16, 64), 1) // 2 == iota((16, 64), 0))
    low = jnp.zeros((16, 128), F32)
    for c in range(3):
        shares = tuple(1.0 if c == k else 0.0 for k in range(3))
        factors = flat_factors((shear, lame, active), steps, (4.0, 4.0, 4.0), shares)
        x, r = flat_smooth(None, restrict(r1, c), factors, steps, True)
        x2[c] = x
        r2[c] = r
        low = low + dot_r(dot_l(own_z, r), to_level3(c))
    send[0] = low
    lane = iota((16, 128), 1)
    low = dot_r(dot_l(own_z, shear), to_level3(0)) + dot_r(dot_l(own_z, lame), to_level3(1))
    low = 0.125 * low
    low = low + ones_where(dot_r(dot_l(own_z, active), to_level3(2)) > 0.5)
    send[1] = low


def spread(v, group):
    lane = iota(v.shape, 1)
    v = jnp.where(lane // 32 == group, v, 0.0)
    back = roll(v, -32 * group, 1)
    return back + roll(back, 32, 1) + roll(back, 64, 1)


def lane_of(v, p):
    return jnp.broadcast_to(v[:, p : p + 1], v.shape)


def eliminate(sources, targets, band, kept):
    rows = [[get(i) for i in range(32)] for get in sources]
    slot = {}
    for p in range(0, 32, 4):
        last = min(32, p + 4 + band)
        for n, a in enumerate(rows):
            r = a[p : p + 4]
            b = [[lane_of(v, p + k) for k in range(4)] for v in r]
            scale = 1.0 / (b[0][0] * b[1][1] - b[0][1] * b[1][0])
            u00, u01, u10, u11 = b[1][1] * scale, b[0][1] * scale, b[1][0] * scale, b[0][0] * scale
            h0 = [u00 * b[0][k] - u01 * b[1][k] for k in (2, 3)]
            h1 = [u11 * b[1][k] - u10 * b[0][k] for k in (2, 3)]
            c2 = [b[2][k + 2] - (b[2][0] * h0[k] + b[2][1] * h1[k]) for k in (0, 1)]
            c3 = [b[3][k + 2] - (b[3][0] * h0[k] + b[3][1] * h1[k]) for k in (0, 1)]
            scale = 1.0 / (c2[0] * c3[1] - c2[1] * c3[0])
            w00, w01, w10, w11 = c3[1] * scale, c2[1] * scale, c3[0] * scale, c2[0] * scale

            def solve(v):
                n0, n1 = u00 * v[0] - u01 * v[1], u11 * v[1] - u10 * v[0]
                v2 = v[2] - (b[2][0] * n0 + b[2][1] * n1)
                v3 = v[3] - (b[3][0] * n0 + b[3][1] * n1)
                n2, n3 = w00 * v2 - w01 * v3, w11 * v3 - w10 * v2
                return [n0 - (h0[0] * n2 + h0[1] * n3), n1 - (h1[0] * n2 + h1[1] * n3), n2, n3]

            new = solve(r)
            for i in range(p + 4, last):
                f = [lane_of(r[k], i) if i - p - k <= band else jnp.zeros((8, 128), F32) for k in range(4)]
                a[i] = a[i] - ((f[0] * new[0] + f[1] * new[1]) + (f[2] * new[2] + f[3] * new[3]))
                at = slot.setdefault((p, i), 4 * len(slot))
                for k, v in enumerate(solve(f)):
                    kept[n, at + k] = v
            a[p : p + 4] = new
    for p in range(24, -1, -4):
        last = min(32, p + 4 + band)
        for n, a in enumerate(rows):
            for k in range(4):
                x = a[p + k]
                for i in range(last - 1, p + 3, -1):
                    x = x - kept[n, slot[p, i] + k] * a[i]
                a[p + k] = x
    for a, put in zip(rows, targets):
        for i in range(32):
            put(i, a[i])


def reader(ref, *at):
    return lambda i: ref[at + (slice(8 * i, 8 * i + 8),)]


def writer(ref, *at):
    def put(i, v):
        ref[at + (slice(8 * i, 8 * i + 8),)] = v

    return put


def one_system(n):
    return pl.ds(n, 32, 8)


def reduced(m, before, after):
    lane = iota((32, 128), 1)
    inner, outer = lane < 32, lane >= 96
    none = jnp.zeros((32, 128), F32)
    left, right = none, none
    if before is not None:
        left = jnp.where(inner, roll(before, 64, 1), jnp.where((lane < 64) | outer, before, 0.0))
    if after is not None:
        right = jnp.where(inner, roll(after, 96, 1), jnp.where(lane >= 64, after, 0.0))
    high, low = split(roll(m, -32, 1))
    both = jnp.where(lane < 64, high.astype(F32), roll(low.astype(F32), 64, 1)).astype(BF16)
    w_high, w_low = split(jnp.concatenate([left, right], axis=0))
    change = mxu(
        jnp.concatenate([both, both], axis=1), jnp.concatenate([w_high, w_high, w_low, w_low], axis=0)
    )
    return jnp.where(inner | outer, m, 0.0) - change


def substitute(get, before, after):
    lane = iota((8, 128), 1)
    v = jnp.where(lane < 96, jnp.where(lane < 64, -before, -after), 1.0)
    v = jnp.where(lane < 32, 0.0, v)
    x = jnp.zeros((8, 128), F32)
    for i in range(32):
        x = jnp.where(lane % 32 == i, jnp.sum(get(i) * v, axis=1, keepdims=True), x)
    return x


def coarse_solve(mods3, rest, rows16, odd, even, solved, low, kept):
    blocks = ones_where(iota((16, 256), 1) // 16 == iota((16, 256), 0))
    shear = 0.0625 * dot_l(blocks, mods3[0])
    lame = 0.0625 * dot_l(blocks, mods3[1])
    active = ones_where(dot_l(blocks, mods3[2]) > 0.5)
    side = dot_l(blocks, rest)
    steps = level3_steps(16)
    scales = (128.0, 128.0, 0.5)
    faces, diag, _ = flat_factors((shear, lame, active), steps, scales, level3_groups(16))
    uppers = []
    for face, (axis, shift, below, above) in zip(faces, steps):
        uppers.append(jnp.where(above, roll(face, -shift, axis), 0.0))
    lane16 = iota((16, 128), 1)
    lane = iota((8, 128), 1)
    sub = iota((8, 128), 0)
    for c in range(3):
        rows16[c, 0] = jnp.where(
            lane16 < 32,
            roll(diag, -32 * c, 1),
            jnp.where(
                lane16 < 64,
                -roll(faces[2], 32 - 32 * c, 1),
                jnp.where(lane16 < 96, -roll(uppers[2], 64 - 32 * c, 1), roll(side, 96 - 32 * c, 1)),
            ),
        )
        for q, v in enumerate((uppers[0], faces[0], uppers[1], faces[1])):
            rows16[c, q + 1] = -roll(v, -32 * c, 1)
    for c in range(3):
        for start, ref in ((0, even), (1, odd)):
            first, x_up, x_down, y_up, y_down = [rows16.at[c, q][pl.ds(start, 8, 2)] for q in range(5)]
            for i in range(32):
                m = jnp.where(lane % 32 == i, first, 0.0)
                for j, v in ((i - 4, x_up), (i + 4, x_down), (i - 1, y_up), (i + 1, y_down)):
                    if 0 <= j < 32:
                        m = jnp.where(lane == j, v, m)
                ref[c, 8 * i : 8 * i + 8] = m
    eliminate([reader(odd, c) for c in range(3)], [writer(odd, c) for c in range(3)], 4, kept)
    inner, outer = lane < 32, lane >= 96
    for c in range(3):
        for i in range(32):
            m = even[c, 8 * i : 8 * i + 8]
            w = odd[c, 8 * i : 8 * i + 8]
            before = roll(w, 1, 0)
            left = jnp.where(inner, roll(before, 64, 1), jnp.where((lane < 64) | outer, before, 0.0))
            right = jnp.where(inner, roll(w, 96, 1), jnp.where(lane >= 64, w, 0.0))
            change = lane_of(m, 32 + i) * left + lane_of(m, 64 + i) * right
            even[c, 8 * i : 8 * i + 8] = jnp.where(inner | outer, m, 0.0) - change
    eliminate([reader(even, c) for c in range(3)], [writer(solved, c) for c in range(3)], 32, kept)
    for c in range(3):
        for n, (to, at) in {0: (1, c), 2: (0, c), 4: (1, 3 + c), 6: (0, 3 + c)}.items():
            before = solved.at[c][one_system(n - 1)] if n > 0 else None
            low.at[to][one_system(at)] = reduced(even.at[c][one_system(n)], before, solved.at[c][one_system(n + 1)])
    eliminate([reader(low, 0)], [writer(low, 0)], 32, kept)
    for c in range(3):
        w4, w12 = low.at[0][one_system(c)], low.at[0][one_system(3 + c)]
        low.at[3][one_system(c)] = reduced(low.at[1][one_system(c)], None, w4)
        low.at[2][one_system(c)] = reduced(low.at[1][one_system(3 + c)], w4, w12)
    eliminate([reader(low, 2)], [writer(low, 2)], 32, kept)
    for c in range(3):
        low.at[4][one_system(c)] = reduced(low.at[3][one_system(c)], None, low.at[2][one_system(c)])
    eliminate([reader(low, 4)], [writer(low, 4)], 32, kept)
    zero = jnp.zeros((8, 128), F32)
    x0 = substitute(reader(low, 4), zero, zero)
    x8 = substitute(reader(low, 2), x0, zero)
    x4 = substitute(reader(low, 0), jnp.where(sub < 3, x0, roll(x8, 3, 0)), jnp.where(sub < 3, x8, 0.0))
    group16 = iota((8, 128), 1) // 32
    all_even, all_odd = zero, zero
    for c in range(3):
        x = zero
        for n, v in ((0, x0[c : c + 1]), (2, x4[c : c + 1]), (4, x8[c : c + 1]), (6, x4[3 + c : 4 + c])):
            x = jnp.where(sub == n, v, x)
        after = jnp.where(sub < 7, roll(x, -1, 0), 0.0)
        x = jnp.where(sub % 2 == 1, substitute(reader(solved, c), roll(x, 1, 0), after), x)
        after = jnp.where(sub < 7, roll(x, -1, 0), 0.0)
        all_even = jnp.where(group16 == c, x, all_even)
        all_odd = jnp.where(group16 == c, substitute(reader(odd, c), x, after), all_odd)
    plane = iota((256, 16), 0) // 16
    place = iota((256, 16), 1)
    place = jnp.where(place < 8, 2 * place, 2 * place - 15)
    return dot_l(ones_where(plane == place), jnp.concatenate([all_even, all_odd], axis=0))


def kernel_c(
    place, got, mod1, x1, r1, mod2, x2, r2, mod0, x0, r0, disp, resid,
    rows16, odd, even, solved, low, kept, e3, e1, faces1, diag1, inv1, d1a, d1b, r1w, faces, diag, inv, d_a, d_b, r_w,
):
    gx, gy, gz = place[0], place[1], place[2]
    b3 = jnp.concatenate([got[k, 0] for k in range(16)], axis=0)
    m3 = jnp.concatenate([got[k, 1] for k in range(16)], axis=0)
    mods3 = tuple(spread(m3, k) for k in range(3))
    steps = level3_steps(256)
    factors = flat_factors(mods3, steps, (8.0, 8.0, 8.0), level3_groups(256))
    x, r = flat_smooth(None, b3, factors, steps, True)
    corr = coarse_solve(mods3, r, rows16, odd, even, solved, low, kept)
    x = x + corr
    r = r - flat_apply(corr, factors, steps)
    x, _ = flat_smooth(x, r, factors, steps, False)
    e3[0:8] = jnp.zeros((8, 128), F32)
    e3[264:272] = jnp.zeros((8, 128), F32)
    e3[8:264] = x
    base = pl.multiple_of(gz * 16, 16)
    own = e3[pl.ds(base + 8, 24)]
    before = e3[pl.ds(base, 8)]
    slab = jnp.concatenate([own, before], axis=0)
    slab = dot_l(ones_where(iota((64, 32), 0) // 2 == iota((64, 32), 1)), slab)
    steps = level2_steps()
    mods = (mod2[0], mod2[1], mod2[2])
    for k in range(3):
        e1[k, 0] = jnp.zeros((16, 128), F32)
        e1[k, 33] = jnp.zeros((16, 128), F32)
        d1a[k, 0] = jnp.zeros((16, 128), F32)
        d1a[k, 33] = jnp.zeros((16, 128), F32)
        d1b[k, 0] = jnp.zeros((16, 128), F32)
        d1b[k, 33] = jnp.zeros((16, 128), F32)
    for k in range(6):
        faces1[k, 33] = jnp.zeros((16, 128), F32)
    up_xy = ones_where(
        ((iota((512, 128), 0) // 32) * 8 + (iota((512, 128), 0) % 16) // 2) == iota((512, 128), 1)
    )
    up_z = ones_where(iota((64, 128), 1) // 2 == iota((64, 128), 0))
    for c in range(3):
        shares = tuple(1.0 if c == k else 0.0 for k in range(3))
        factors = flat_factors(mods, steps, (4.0, 4.0, 4.0), shares)
        corr = dot_r_nt(slab, to_level3(c))
        x = x2[c] + corr
        r = r2[c] - flat_apply(corr, factors, steps)
        x, _ = flat_smooth(x, r, factors, steps, False)
        lifted = dot_l(up_xy, dot_r(x.T, up_z))
        for j in range(32):
            e1[c, j + 1] = lifted[16 * j : 16 * j + 16]
    plane_factors(mod1, 2.0, faces1, diag1, inv1, 1, 33, True)
    plane_sweep(e1, d1a, r1, r1w, faces1, diag1, inv1, 1, 33, START)
    for c in range(3):
        e1[c, 1:33] = e1[c, 1:33] + x1[c, 1:33] + d1a[c, 1:33]
    plane_sweep(d1a, d1b, r1w, r1w, faces1, diag1, inv1, 1, 33, CHEB[0])
    for c in range(3):
        e1[c, 1:33] = e1[c, 1:33] + d1b[c, 1:33]
    plane_sweep(d1b, d1a, r1w, None, faces1, diag1, inv1, 1, 33, CHEB[1])
    for c in range(3):
        e1[c, 1:33] = e1[c, 1:33] + d1a[c, 1:33]
    row = iota((24, 16), 0)
    row = jnp.where(row >= 16, row - 24, row)
    up_y = ones_where((row + 8 * gy + 16) // 2 - 8 == iota((24, 16), 1))
    up_z0 = ones_where(iota((128, 256), 1) // 2 == iota((128, 256), 0))
    planes = []
    for c in range(3):
        for j in range(8):
            planes.append(e1[c, jnp.clip(4 * gx + (j - 1), 0, 33)])
    lifted = dot_r(jnp.concatenate(planes, axis=0), up_z0)
    up_y = jnp.concatenate([up_y, up_y], axis=1).astype(BF16)
    for c in range(3):
        for j in range(8):
            at = 16 * (8 * c + j)
            high, low = split(lifted[at : at + 16])
            plane = mxu(up_y, jnp.concatenate([high, low], axis=0))
            d_b[c, 3 + 2 * j] = plane
            d_b[c, 4 + 2 * j] = plane
    plane_factors(mod0, 1.0, faces, diag, inv, 4, 19, False)
    own_part = (slice(7, 15), slice(0, 8), slice(0, 128))
    for c in range(3):
        disp[c] = x0[c] + d_b[(c,) + own_part]
    plane_sweep(d_b, d_a, r0, r_w, faces, diag, inv, 4, 18, START, 4, 0)
    for c in range(3):
        disp[c] = disp[c] + d_a[(c,) + own_part]
    plane_sweep(d_a, d_b, r_w, r_w, faces, diag, inv, 5, 17, CHEB[0])
    for c in range(3):
        disp[c] = disp[c] + d_b[(c,) + own_part]
    plane_sweep(d_b, d_a, r_w, r_w, faces, diag, inv, 6, 16, CHEB[1])
    for c in range(3):
        disp[c] = disp[c] + d_a[(c,) + own_part]
    plane_sweep(d_a, None, r_w, r_w, faces, diag, inv, 7, 15, None)
    for c in range(3):
        resid[c] = r_w[(c,) + own_part]


IN_VMEM = pl.BlockSpec(memory_space=pltpu.VMEM)
IN_SMEM = pl.BlockSpec(memory_space=pltpu.SMEM)


def shaped(*shape):
    return jax.ShapeDtypeStruct(shape, F32)


def scratch(*shape):
    return pltpu.VMEM(shape, F32)


PARAMS = dict(compiler_params=pltpu.CompilerParams(vmem_limit_bytes=VMEM_LIMIT))


def call_a(moduli, ext):
    return pl.pallas_call(
        kernel_a,
        out_shape=(shaped(80, 128), shaped(3, 14, 24, 256), shaped(3, 8, 8, 128), shaped(3, 22, 24, 256)),
        in_specs=[IN_SMEM, IN_VMEM],
        out_specs=(IN_VMEM,) * 4,
        scratch_shapes=[scratch(6, 22, 24, 256)] + [scratch(3, 22, 24, 256)] * 5,
        **PARAMS,
    )(moduli, ext)


def call_b(got):
    one, two = (3, 34, 16, 128), (3, 64, 128)
    return pl.pallas_call(
        kernel_b,
        out_shape=(shaped(2, 16, 128),) + (shaped(*one),) * 3 + (shaped(*two),) * 3,
        in_specs=[IN_VMEM],
        out_specs=(IN_VMEM,) * 7,
        scratch_shapes=[scratch(6, 34, 16, 128)] + [scratch(*one)] * 5,
        **PARAMS,
    )(got)


def call_c(place, got, level1, level2, level0):
    one, zero = (3, 34, 16, 128), (3, 22, 24, 256)
    return pl.pallas_call(
        kernel_c,
        out_shape=(shaped(3, 8, 8, 128), shaped(3, 8, 8, 128)),
        in_specs=[IN_SMEM] + [IN_VMEM] * 10,
        out_specs=(IN_VMEM,) * 2,
        scratch_shapes=[scratch(3, 5, 16, 128)] + [scratch(3, 256, 128)] * 3
        + [scratch(5, 256, 128), scratch(3, 448, 8, 128), scratch(272, 128), scratch(*one)]
        + [scratch(6, 34, 16, 128)] + [scratch(*one)] * 5
        + [scratch(6, 22, 24, 256)] + [scratch(*zero)] * 5,
        **PARAMS,
    )(place, got, *level1, *level2, *level0)


def both_ways(to_next, to_before, axis):
    count = lax.axis_size(axis)
    up = [(i, i + 1) for i in range(count - 1)]
    down = [(j, i) for i, j in up]
    return lax.ppermute(to_next, axis, up), lax.ppermute(to_before, axis, down)


def extend(body_forces, material, fixed_mask):
    cells = jnp.concatenate(
        [body_forces, (material + 1).astype(F32)[None], (1 - fixed_mask).astype(F32)[None]], axis=0
    )
    before, after = both_ways(cells, cells, "gz")
    halo = jnp.where(iota((1, 1, 1, 128), 3) < 64, after, before)
    cells = jnp.concatenate([cells, halo], axis=3)
    before, after = both_ways(cells[:, 1:8], cells[:, 0:7], "gx")
    cells = jnp.concatenate([before, cells, after], axis=1)
    before, after = both_ways(cells, cells, "gy")
    return jnp.concatenate([cells, after, before], axis=2)


def to_all(block, axes, count):
    copies = jnp.broadcast_to(block[None], (count,) + block.shape)
    return lax.all_to_all(copies, axes, 0, 0, tiled=True)


def body(body_forces, material, fixed_mask, moduli):
    ext = extend(body_forces, material, fixed_mask)
    send, r0, x0, mod0 = call_a(moduli, ext)
    send, mod1, x1, r1, mod2, x2, r2 = call_b(to_all(send, ("gx", "gy"), 32))
    got = to_all(send, "gz", 16)
    place = jnp.stack([lax.axis_index("gx"), lax.axis_index("gy"), lax.axis_index("gz")]).astype(jnp.int32)
    return call_c(place, got, (mod1, x1, r1), (mod2, x2, r2), (mod0, x0, r0))


def solution(mesh):
    cells = P(None, "gx", "gy", "gz")
    part = P("gx", "gy", "gz")
    return jax.shard_map(
        body, mesh=mesh, in_specs=(cells, part, part, P()), out_specs=(cells, cells), check_vma=False
    )
```

```python
import jax
import jax.numpy as jnp
from jax import lax
from jax.experimental import pallas as pl
from jax.experimental.pallas import tpu as pltpu
from jax.sharding import PartitionSpec as P

F32 = jnp.float32
CLASSES = 16
THETA = 1.125
HALF = 0.875
SIGMA = THETA / HALF
VMEM_LIMIT = 36 * 1024 * 1024


def cheb_factors():
    rho = 1.0 / SIGMA
    found = []
    for _ in range(2):
        rho_next = 1.0 / (2.0 * SIGMA - rho)
        found.append((rho_next * rho, 2.0 * rho_next / HALF))
        rho = rho_next
    return found


CHEB = cheb_factors()
START = (0.0, 1.0 / THETA)


BF16 = jnp.bfloat16


def split(v):
    high = v.astype(BF16)
    return high, (v - high.astype(F32)).astype(BF16)


def mxu(a, b, b_dim=0):
    return lax.dot_general(a, b, (((1,), (b_dim,)), ((), ())), preferred_element_type=F32)


def dot_l(picks, v):
    high, low = split(v)
    picks = picks.astype(BF16)
    return mxu(picks, high) + mxu(picks, low)


def dot_r(v, picks):
    high, low = split(v)
    picks = picks.astype(BF16)
    return mxu(high, picks) + mxu(low, picks)


def dot_l_nt(picks, v):
    high, low = split(v)
    picks = picks.astype(BF16)
    return mxu(picks, high, 1) + mxu(picks, low, 1)


def dot_r_nt(v, picks):
    high, low = split(v)
    picks = picks.astype(BF16)
    return mxu(high, picks, 1) + mxu(low, picks, 1)


def iota(shape, dim):
    return lax.broadcasted_iota(jnp.int32, shape, dim)


def ones_where(cond):
    return jnp.where(cond, 1.0, 0.0).astype(F32)


def roll(v, shift, axis):
    size = v.shape[axis]
    return pltpu.roll(v, shift % size, axis)


def loop(lo, hi, body):
    count = hi - lo
    step = max(k for k in (1, 2, 3, 4, 5) if count % k == 0)

    def several(n, carry):
        for k in range(step):
            body(lo + n * step + k)
        return carry

    lax.fori_loop(0, count // step, several, 0)


def neighbours_y(v, rows_masked):
    down, up = roll(v, 1, 0), roll(v, -1, 0)
    if rows_masked:
        row = iota(v.shape, 0)
        down = jnp.where(row >= 1, down, 0.0)
        up = jnp.where(row <= v.shape[0] - 2, up, 0.0)
    return down, up


def plane_factors(mod, scale, faces, diag, inv, lo, hi, rows_masked):
    half = 0.5 * scale

    def body(i):
        def fields(j):
            shear, lame = mod[0, j], mod[1, j]
            return half * shear, half * (shear + lame)

        p, g = fields(i)
        pm, gm = fields(i - 1)
        pp, gp = fields(i + 1)
        a, am = mod[2, i], mod[2, i - 1]
        pyd, pyu = neighbours_y(p, rows_masked)
        gyd, gyu = neighbours_y(g, rows_masked)
        ayd, _ = neighbours_y(a, rows_masked)
        pzd, pzu = roll(p, 1, 1), roll(p, -1, 1)
        gzd, gzu = roll(g, 1, 1), roll(g, -1, 1)
        azd = roll(a, 1, 1)
        base = (pm + pp) + (pyd + pyu) + (pzd + pzu) + 6.0 * p
        extra = (gm + gp, gyd + gyu, gzd + gzu)
        for c in range(3):
            d = a * (base + (extra[c] + 2.0 * g)) + (1.0 - a)
            diag[c, i] = d
            inv[c, i] = 1.0 / d
        for k, (pn, gn, an) in enumerate(((pm, gm, am), (pyd, gyd, ayd), (pzd, gzd, azd))):
            both = a * an
            face = p + pn
            faces[2 * k, i] = both * face
            faces[2 * k + 1, i] = both * (face + (g + gn))

    loop(lo, hi, body)


def plane_sweep(d, d_next, r_in, r_out, faces, diag, inv, lo, hi, pair, r_in_at=0, r_out_at=0):
    def body(i):
        for c in range(3):
            fx = faces[1 if c == 0 else 0, i]
            fxu = faces[1 if c == 0 else 0, i + 1]
            fy = faces[3 if c == 1 else 2, i]
            fz = faces[5 if c == 2 else 4, i]
            dc = d[c, i]
            t = fx * d[c, i - 1] + fxu * d[c, i + 1]
            t = t + (fy * roll(dc, 1, 0) + roll(fy * dc, -1, 0))
            t = t + (fz * roll(dc, 1, 1) + roll(fz * dc, -1, 1))
            r = r_in[c, i - r_in_at] - (diag[c, i] * dc - t)
            if r_out is not None:
                r_out[c, i - r_out_at] = r
            if pair is not None:
                new = (pair[1] * inv[c, i]) * r
                if pair[0] != 0.0:
                    new = new + pair[0] * dc
                d_next[c, i] = new

    loop(lo, hi, body)


def kernel_a(moduli, ext, send, r_out, x_out, mod, faces, diag, inv, d_a, d_b, r):
    def look_up(i):
        mat = ext[3, i]
        shear = jnp.zeros(mat.shape, F32)
        lame = jnp.zeros(mat.shape, F32)
        for k in range(CLASSES):
            hit = mat == float(k + 1)
            shear = jnp.where(hit, moduli[0, k], shear)
            lame = jnp.where(hit, moduli[1, k], lame)
        mod[0, i] = shear
        mod[1, i] = lame
        mod[2, i] = ext[4, i]

    loop(0, 16, look_up)
    for k in range(3):
        mod[k, 16] = jnp.zeros((16, 256), F32)
    plane_factors(mod, 1.0, faces, diag, inv, 1, 15, False)

    def start(i):
        for c in range(3):
            d_a[c, i] = (START[1] * inv[c, i]) * ext[c, i]

    loop(1, 15, start)
    plane_sweep(d_a, d_b, ext, r, faces, diag, inv, 2, 14, CHEB[0])
    for c in range(3):
        x_out[c] = d_a[c, 4:12, 0:8, 0:128] + d_b[c, 4:12, 0:8, 0:128]
    plane_sweep(d_b, d_a, r, r, faces, diag, inv, 3, 13, CHEB[1])
    for c in range(3):
        x_out[c] = x_out[c] + d_a[c, 4:12, 0:8, 0:128]
    plane_sweep(d_a, None, r, r, faces, diag, inv, 4, 12, None)
    for c in range(3):
        r_out[c] = r[c, 4:12, 0:8]
    rows = []
    for c in range(3):
        for j in range(4):
            rows.append(r_out[c, 2 * j] + r_out[c, 2 * j + 1])
    for k in range(3):
        for j in range(4):
            rows.append(mod[k, 4 + 2 * j, 0:8] + mod[k, 5 + 2 * j, 0:8])
    stacked = jnp.concatenate(rows, axis=0)
    pair_z = ones_where(iota((256, 128), 0) // 2 == iota((256, 128), 1))
    pair_y = ones_where(iota((96, 192), 1) // 2 == iota((96, 192), 0))
    low = dot_l(pair_y, dot_r(stacked, pair_z))
    row = iota((96, 128), 0)
    low = jnp.where(row < 48, low, jnp.where(row < 80, 0.125 * low, ones_where(low > 0.5)))
    lane = iota((48, 128), 1)
    send[0:48] = jnp.where(lane < 64, low[0:48], roll(low[48:96], 64, 1))
    lane = iota((32, 128), 1)
    packed = jnp.zeros((32, 128), F32)
    for k in range(3):
        part = low[32 * k : 32 * k + 32]
        packed = jnp.where((lane >= 40 * k) & (lane < 40 * k + 20), roll(part, 40 * k - 64, 1), packed)
        packed = jnp.where((lane >= 40 * k + 20) & (lane < 40 * k + 40), roll(part, 40 * k - 88, 1), packed)
    send[48:80] = packed


def flat_factors(mods, steps, scales, groups):
    shear, lame, a = mods
    total = 0.0
    faces = []
    for (axis, shift, below, above), scale, share in zip(steps, scales, groups):
        h = (0.5 * scale) * (shear + share * (shear + lame))
        dn, up = roll(h, shift, axis), roll(h, -shift, axis)
        an = roll(a, shift, axis)
        if below is not None:
            dn = jnp.where(below, dn, 0.0)
            up = jnp.where(above, up, 0.0)
            an = jnp.where(below, an, 0.0)
        total = total + (2.0 * h + (dn + up))
        faces.append((a * an) * (h + dn))
    diag = a * total + (1.0 - a)
    return faces, diag, 1.0 / diag


def flat_apply(v, factors, steps):
    faces, diag, inv = factors
    out = diag * v
    for face, (axis, shift, below, above) in zip(faces, steps):
        out = out - (face * roll(v, shift, axis) + roll(face * v, -shift, axis))
    return out


def flat_smooth(x, r, factors, steps, last):
    inv = factors[2]
    d = (START[1] * inv) * r
    for sweep in range(3):
        x = d if x is None else x + d
        if sweep == 2 and not last:
            return x, None
        r = r - flat_apply(d, factors, steps)
        if sweep < 2:
            c1, c2 = CHEB[sweep]
            d = c1 * d + (c2 * inv) * r
    return x, r


def level2_steps():
    lane = iota((64, 128), 1)
    return (
        (1, 8, lane >= 8, lane < 120),
        (1, 1, lane % 8 >= 1, lane % 8 <= 6),
        (0, 1, None, None),
    )


def level3_steps(rows):
    lane = iota((rows, 128), 1)
    row = iota((rows, 128), 0)
    return (
        (1, 4, lane % 32 >= 4, lane % 32 < 28),
        (1, 1, lane % 4 >= 1, lane % 4 <= 2),
        (0, 1, row >= 1, row <= rows - 2),
    )


def level3_groups(rows):
    group = iota((rows, 128), 1) // 32
    return tuple(ones_where(group == k) for k in range(3))


def to_level3(k):
    cell = iota((128, 128), 0)
    lane = iota((128, 128), 1)
    return ones_where(lane == 32 * k + (cell // 16) * 4 + (cell % 8) // 2)


def kernel_b(got, send, mod1, x1, r1, mod2, x2, r2, faces, diag, inv, d_a, d_b, b1):
    sub = iota((8, 128), 0) < 4
    zero = jnp.zeros((16, 128), F32)
    for k in range(3):
        mod1[k, 0] = zero
        mod1[k, 33] = zero
        d_a[k, 0] = zero
        d_a[k, 33] = zero
        d_b[k, 0] = zero
        d_b[k, 33] = zero
    for k in range(6):
        faces[k, 33] = zero

    lane = iota((8, 128), 1)

    def tile(dev, t):
        own = got[dev, 8 * (t % 6) : 8 * (t % 6) + 8]
        if t >= 6:
            own = roll(own, 64, 1)
        halo = got[dev, 48 + 8 * (t % 4) : 56 + 8 * (t % 4)]
        after = roll(halo, 64 - 40 * (t // 4), 1)
        before = roll(halo, 88 - 40 * (t // 4), 1)
        halo = jnp.where(lane < 84, after, jnp.where(lane >= 108, before, 0.0))
        return jnp.where(lane < 64, own, halo)

    def unpack(gx, carry):
        for f in range(6):
            for pair in range(2):
                at = f * 2 + pair
                for half in range(2):
                    s0 = tile(gx * 4 + 2 * half, at)
                    s1 = tile(gx * 4 + 2 * half + 1, at)
                    even = jnp.where(sub, s0, roll(s1, 4, 0))
                    odd = jnp.where(sub, roll(s0, 4, 0), s1)
                    x = gx * 4 + 2 * pair + 1
                    rows = slice(8 * half, 8 * half + 8)
                    if f < 3:
                        b1[f, x, rows] = even
                        b1[f, x + 1, rows] = odd
                    else:
                        mod1[f - 3, x, rows] = even
                        mod1[f - 3, x + 1, rows] = odd
        return carry

    lax.fori_loop(0, 8, unpack, 0)
    plane_factors(mod1, 2.0, faces, diag, inv, 1, 33, True)

    def start(i):
        for c in range(3):
            d_a[c, i] = (START[1] * inv[c, i]) * b1[c, i]

    loop(1, 33, start)
    plane_sweep(d_a, d_b, b1, r1, faces, diag, inv, 1, 33, CHEB[0])
    for c in range(3):
        x1[c] = d_a[c] + d_b[c]
    plane_sweep(d_b, d_a, r1, r1, faces, diag, inv, 1, 33, CHEB[1])
    for c in range(3):
        x1[c] = x1[c] + d_a[c]
    plane_sweep(d_a, None, r1, r1, faces, diag, inv, 1, 33, None)

    pair_y = ones_where(iota((128, 256), 1) // 2 == iota((128, 256), 0))
    pair_z = ones_where(iota((64, 128), 1) // 2 == iota((64, 128), 0))

    def restrict(ref, k):
        planes = [ref[k, 1 + 2 * j] + ref[k, 2 + 2 * j] for j in range(16)]
        return dot_l_nt(pair_z, dot_l(pair_y, jnp.concatenate(planes, axis=0)))

    shear = 0.125 * restrict(mod1, 0)
    lame = 0.125 * restrict(mod1, 1)
    active = ones_where(restrict(mod1, 2) > 0.5)
    mod2[0] = shear
    mod2[1] = lame
    mod2[2] = active
    steps = level2_steps()
    own_z = ones_where(iota((16, 64), 1) // 2 == iota((16, 64), 0))
    low = jnp.zeros((16, 128), F32)
    for c in range(3):
        shares = tuple(1.0 if c == k else 0.0 for k in range(3))
        factors = flat_factors((shear, lame, active), steps, (4.0, 4.0, 4.0), shares)
        x, r = flat_smooth(None, restrict(r1, c), factors, steps, True)
        x2[c] = x
        r2[c] = r
        low = low + dot_r(dot_l(own_z, r), to_level3(c))
    send[0] = low
    lane = iota((16, 128), 1)
    low = dot_r(dot_l(own_z, shear), to_level3(0)) + dot_r(dot_l(own_z, lame), to_level3(1))
    low = 0.125 * low
    low = low + ones_where(dot_r(dot_l(own_z, active), to_level3(2)) > 0.5)
    send[1] = low


def spread(v, group):
    lane = iota(v.shape, 1)
    v = jnp.where(lane // 32 == group, v, 0.0)
    back = roll(v, -32 * group, 1)
    return back + roll(back, 32, 1) + roll(back, 64, 1)


def lane_of(v, p):
    return jnp.broadcast_to(v[:, p : p + 1], v.shape)


def eliminate(sources, targets, band, kept):
    rows = [[get(i) for i in range(32)] for get in sources]
    slot = {}
    for p in range(0, 32, 4):
        last = min(32, p + 4 + band)
        for n, a in enumerate(rows):
            r = a[p : p + 4]
            b = [[lane_of(v, p + k) for k in range(4)] for v in r]
            scale = 1.0 / (b[0][0] * b[1][1] - b[0][1] * b[1][0])
            u00, u01, u10, u11 = b[1][1] * scale, b[0][1] * scale, b[1][0] * scale, b[0][0] * scale
            h0 = [u00 * b[0][k] - u01 * b[1][k] for k in (2, 3)]
            h1 = [u11 * b[1][k] - u10 * b[0][k] for k in (2, 3)]
            c2 = [b[2][k + 2] - (b[2][0] * h0[k] + b[2][1] * h1[k]) for k in (0, 1)]
            c3 = [b[3][k + 2] - (b[3][0] * h0[k] + b[3][1] * h1[k]) for k in (0, 1)]
            scale = 1.0 / (c2[0] * c3[1] - c2[1] * c3[0])
            w00, w01, w10, w11 = c3[1] * scale, c2[1] * scale, c3[0] * scale, c2[0] * scale

            def solve(v):
                n0, n1 = u00 * v[0] - u01 * v[1], u11 * v[1] - u10 * v[0]
                v2 = v[2] - (b[2][0] * n0 + b[2][1] * n1)
                v3 = v[3] - (b[3][0] * n0 + b[3][1] * n1)
                n2, n3 = w00 * v2 - w01 * v3, w11 * v3 - w10 * v2
                return [n0 - (h0[0] * n2 + h0[1] * n3), n1 - (h1[0] * n2 + h1[1] * n3), n2, n3]

            new = solve(r)
            for i in range(p + 4, last):
                f = [lane_of(r[k], i) if i - p - k <= band else jnp.zeros((8, 128), F32) for k in range(4)]
                a[i] = a[i] - ((f[0] * new[0] + f[1] * new[1]) + (f[2] * new[2] + f[3] * new[3]))
                at = slot.setdefault((p, i), 4 * len(slot))
                for k, v in enumerate(solve(f)):
                    kept[n, at + k] = v
            a[p : p + 4] = new
    for p in range(24, -1, -4):
        last = min(32, p + 4 + band)
        for n, a in enumerate(rows):
            for k in range(4):
                x = a[p + k]
                for i in range(last - 1, p + 3, -1):
                    x = x - kept[n, slot[p, i] + k] * a[i]
                a[p + k] = x
    for a, put in zip(rows, targets):
        for i in range(32):
            put(i, a[i])


def reader(ref, *at):
    return lambda i: ref[at + (slice(8 * i, 8 * i + 8),)]


def writer(ref, *at):
    def put(i, v):
        ref[at + (slice(8 * i, 8 * i + 8),)] = v

    return put


def one_system(n):
    return pl.ds(n, 32, 8)


def reduced(m, before, after):
    lane = iota((32, 128), 1)
    inner, outer = lane < 32, lane >= 96
    none = jnp.zeros((32, 128), F32)
    left, right = none, none
    if before is not None:
        left = jnp.where(inner, roll(before, 64, 1), jnp.where((lane < 64) | outer, before, 0.0))
    if after is not None:
        right = jnp.where(inner, roll(after, 96, 1), jnp.where(lane >= 64, after, 0.0))
    high, low = split(roll(m, -32, 1))
    both = jnp.where(lane < 64, high.astype(F32), roll(low.astype(F32), 64, 1)).astype(BF16)
    w_high, w_low = split(jnp.concatenate([left, right], axis=0))
    change = mxu(
        jnp.concatenate([both, both], axis=1), jnp.concatenate([w_high, w_high, w_low, w_low], axis=0)
    )
    return jnp.where(inner | outer, m, 0.0) - change


def substitute(get, before, after):
    lane = iota((8, 128), 1)
    v = jnp.where(lane < 96, jnp.where(lane < 64, -before, -after), 1.0)
    v = jnp.where(lane < 32, 0.0, v)
    x = jnp.zeros((8, 128), F32)
    for i in range(32):
        x = jnp.where(lane % 32 == i, jnp.sum(get(i) * v, axis=1, keepdims=True), x)
    return x


def coarse_solve(mods3, rest, rows16, odd, even, solved, low, kept):
    blocks = ones_where(iota((16, 256), 1) // 16 == iota((16, 256), 0))
    shear = 0.0625 * dot_l(blocks, mods3[0])
    lame = 0.0625 * dot_l(blocks, mods3[1])
    active = ones_where(dot_l(blocks, mods3[2]) > 0.5)
    side = dot_l(blocks, rest)
    steps = level3_steps(16)
    scales = (128.0, 128.0, 0.5)
    faces, diag, _ = flat_factors((shear, lame, active), steps, scales, level3_groups(16))
    uppers = []
    for face, (axis, shift, below, above) in zip(faces, steps):
        uppers.append(jnp.where(above, roll(face, -shift, axis), 0.0))
    lane16 = iota((16, 128), 1)
    lane = iota((8, 128), 1)
    sub = iota((8, 128), 0)
    for c in range(3):
        rows16[c, 0] = jnp.where(
            lane16 < 32,
            roll(diag, -32 * c, 1),
            jnp.where(
                lane16 < 64,
                -roll(faces[2], 32 - 32 * c, 1),
                jnp.where(lane16 < 96, -roll(uppers[2], 64 - 32 * c, 1), roll(side, 96 - 32 * c, 1)),
            ),
        )
        for q, v in enumerate((uppers[0], faces[0], uppers[1], faces[1])):
            rows16[c, q + 1] = -roll(v, -32 * c, 1)
    for c in range(3):
        for start, ref in ((0, even), (1, odd)):
            first, x_up, x_down, y_up, y_down = [rows16.at[c, q][pl.ds(start, 8, 2)] for q in range(5)]
            for i in range(32):
                m = jnp.where(lane % 32 == i, first, 0.0)
                for j, v in ((i - 4, x_up), (i + 4, x_down), (i - 1, y_up), (i + 1, y_down)):
                    if 0 <= j < 32:
                        m = jnp.where(lane == j, v, m)
                ref[c, 8 * i : 8 * i + 8] = m
    eliminate([reader(odd, c) for c in range(3)], [writer(odd, c) for c in range(3)], 4, kept)
    inner, outer = lane < 32, lane >= 96
    for c in range(3):
        for i in range(32):
            m = even[c, 8 * i : 8 * i + 8]
            w = odd[c, 8 * i : 8 * i + 8]
            before = roll(w, 1, 0)
            left = jnp.where(inner, roll(before, 64, 1), jnp.where((lane < 64) | outer, before, 0.0))
            right = jnp.where(inner, roll(w, 96, 1), jnp.where(lane >= 64, w, 0.0))
            change = lane_of(m, 32 + i) * left + lane_of(m, 64 + i) * right
            even[c, 8 * i : 8 * i + 8] = jnp.where(inner | outer, m, 0.0) - change
    eliminate([reader(even, c) for c in range(3)], [writer(solved, c) for c in range(3)], 32, kept)
    for c in range(3):
        for n, (to, at) in {0: (1, c), 2: (0, c), 4: (1, 3 + c), 6: (0, 3 + c)}.items():
            before = solved.at[c][one_system(n - 1)] if n > 0 else None
            low.at[to][one_system(at)] = reduced(even.at[c][one_system(n)], before, solved.at[c][one_system(n + 1)])
    eliminate([reader(low, 0)], [writer(low, 0)], 32, kept)
    for c in range(3):
        w4, w12 = low.at[0][one_system(c)], low.at[0][one_system(3 + c)]
        low.at[3][one_system(c)] = reduced(low.at[1][one_system(c)], None, w4)
        low.at[2][one_system(c)] = reduced(low.at[1][one_system(3 + c)], w4, w12)
    eliminate([reader(low, 2)], [writer(low, 2)], 32, kept)
    for c in range(3):
        low.at[4][one_system(c)] = reduced(low.at[3][one_system(c)], None, low.at[2][one_system(c)])
    eliminate([reader(low, 4)], [writer(low, 4)], 32, kept)
    zero = jnp.zeros((8, 128), F32)
    x0 = substitute(reader(low, 4), zero, zero)
    x8 = substitute(reader(low, 2), x0, zero)
    x4 = substitute(reader(low, 0), jnp.where(sub < 3, x0, roll(x8, 3, 0)), jnp.where(sub < 3, x8, 0.0))
    group16 = iota((8, 128), 1) // 32
    all_even, all_odd = zero, zero
    for c in range(3):
        x = zero
        for n, v in ((0, x0[c : c + 1]), (2, x4[c : c + 1]), (4, x8[c : c + 1]), (6, x4[3 + c : 4 + c])):
            x = jnp.where(sub == n, v, x)
        after = jnp.where(sub < 7, roll(x, -1, 0), 0.0)
        x = jnp.where(sub % 2 == 1, substitute(reader(solved, c), roll(x, 1, 0), after), x)
        after = jnp.where(sub < 7, roll(x, -1, 0), 0.0)
        all_even = jnp.where(group16 == c, x, all_even)
        all_odd = jnp.where(group16 == c, substitute(reader(odd, c), x, after), all_odd)
    plane = iota((256, 16), 0) // 16
    place = iota((256, 16), 1)
    place = jnp.where(place < 8, 2 * place, 2 * place - 15)
    return dot_l(ones_where(plane == place), jnp.concatenate([all_even, all_odd], axis=0))


def kernel_c(
    place, got, mod1, x1, r1, mod2, x2, r2, mod0, x0, r0, disp, resid,
    rows16, odd, even, solved, low, kept, e3, e1, faces1, diag1, inv1, d1a, d1b, r1w, faces, diag, inv, d_a, d_b, r_w,
):
    gx, gy, gz = place[0], place[1], place[2]
    b3 = jnp.concatenate([got[k, 0] for k in range(16)], axis=0)
    m3 = jnp.concatenate([got[k, 1] for k in range(16)], axis=0)
    mods3 = tuple(spread(m3, k) for k in range(3))
    steps = level3_steps(256)
    factors = flat_factors(mods3, steps, (8.0, 8.0, 8.0), level3_groups(256))
    x, r = flat_smooth(None, b3, factors, steps, True)
    corr = coarse_solve(mods3, r, rows16, odd, even, solved, low, kept)
    x = x + corr
    r = r - flat_apply(corr, factors, steps)
    x, _ = flat_smooth(x, r, factors, steps, False)
    e3[0:8] = jnp.zeros((8, 128), F32)
    e3[264:272] = jnp.zeros((8, 128), F32)
    e3[8:264] = x
    base = pl.multiple_of(gz * 16, 16)
    own = e3[pl.ds(base + 8, 24)]
    before = e3[pl.ds(base, 8)]
    slab = jnp.concatenate([own, before], axis=0)
    slab = dot_l(ones_where(iota((64, 32), 0) // 2 == iota((64, 32), 1)), slab)
    steps = level2_steps()
    mods = (mod2[0], mod2[1], mod2[2])
    for k in range(3):
        e1[k, 0] = jnp.zeros((16, 128), F32)
        e1[k, 33] = jnp.zeros((16, 128), F32)
        d1a[k, 0] = jnp.zeros((16, 128), F32)
        d1a[k, 33] = jnp.zeros((16, 128), F32)
        d1b[k, 0] = jnp.zeros((16, 128), F32)
        d1b[k, 33] = jnp.zeros((16, 128), F32)
    for k in range(6):
        faces1[k, 33] = jnp.zeros((16, 128), F32)
    up_xy = ones_where(
        ((iota((512, 128), 0) // 32) * 8 + (iota((512, 128), 0) % 16) // 2) == iota((512, 128), 1)
    )
    up_z = ones_where(iota((64, 128), 1) // 2 == iota((64, 128), 0))
    for c in range(3):
        shares = tuple(1.0 if c == k else 0.0 for k in range(3))
        factors = flat_factors(mods, steps, (4.0, 4.0, 4.0), shares)
        corr = dot_r_nt(slab, to_level3(c))
        x = x2[c] + corr
        r = r2[c] - flat_apply(corr, factors, steps)
        x, _ = flat_smooth(x, r, factors, steps, False)
        lifted = dot_l(up_xy, dot_r(x.T, up_z))
        for j in range(32):
            e1[c, j + 1] = lifted[16 * j : 16 * j + 16]
    plane_factors(mod1, 2.0, faces1, diag1, inv1, 1, 33, True)
    plane_sweep(e1, d1a, r1, r1w, faces1, diag1, inv1, 1, 33, START)
    for c in range(3):
        e1[c, 1:33] = e1[c, 1:33] + x1[c, 1:33] + d1a[c, 1:33]
    plane_sweep(d1a, d1b, r1w, r1w, faces1, diag1, inv1, 1, 33, CHEB[0])
    for c in range(3):
        e1[c, 1:33] = e1[c, 1:33] + d1b[c, 1:33]
    plane_sweep(d1b, d1a, r1w, None, faces1, diag1, inv1, 1, 33, CHEB[1])
    for c in range(3):
        e1[c, 1:33] = e1[c, 1:33] + d1a[c, 1:33]
    row = iota((16, 16), 0)
    row = jnp.where(row >= 12, row - 16, row)
    up_y = ones_where((row + 8 * gy + 16) // 2 - 8 == iota((16, 16), 1))
    up_z0 = ones_where(iota((128, 256), 1) // 2 == iota((128, 256), 0))
    planes = []
    for c in range(3):
        for j in range(8):
            planes.append(e1[c, jnp.clip(4 * gx + (j - 1), 0, 33)])
    lifted = dot_r(jnp.concatenate(planes, axis=0), up_z0)
    up_y = jnp.concatenate([up_y, up_y], axis=1).astype(BF16)
    for c in range(3):
        for j in range(8):
            at = 16 * (8 * c + j)
            high, low = split(lifted[at : at + 16])
            plane = mxu(up_y, jnp.concatenate([high, low], axis=0))
            d_b[c, 2 * j] = plane
            d_b[c, 2 * j + 1] = plane
    plane_factors(mod0, 1.0, faces, diag, inv, 1, 16, False)
    own_part = (slice(4, 12), slice(0, 8), slice(0, 128))
    for c in range(3):
        disp[c] = x0[c] + d_b[(c,) + own_part]
    plane_sweep(d_b, d_a, r0, r_w, faces, diag, inv, 1, 15, START, 1, 0)
    for c in range(3):
        disp[c] = disp[c] + d_a[(c,) + own_part]
    plane_sweep(d_a, d_b, r_w, r_w, faces, diag, inv, 2, 14, CHEB[0])
    for c in range(3):
        disp[c] = disp[c] + d_b[(c,) + own_part]
    plane_sweep(d_b, d_a, r_w, r_w, faces, diag, inv, 3, 13, CHEB[1])
    for c in range(3):
        disp[c] = disp[c] + d_a[(c,) + own_part]
    plane_sweep(d_a, None, r_w, r_w, faces, diag, inv, 4, 12, None)
    for c in range(3):
        resid[c] = r_w[(c,) + own_part]


IN_VMEM = pl.BlockSpec(memory_space=pltpu.VMEM)
IN_SMEM = pl.BlockSpec(memory_space=pltpu.SMEM)


def shaped(*shape):
    return jax.ShapeDtypeStruct(shape, F32)


def scratch(*shape):
    return pltpu.VMEM(shape, F32)


PARAMS = dict(compiler_params=pltpu.CompilerParams(vmem_limit_bytes=VMEM_LIMIT))


def call_a(moduli, ext):
    return pl.pallas_call(
        kernel_a,
        out_shape=(shaped(80, 128), shaped(3, 8, 8, 256), shaped(3, 8, 8, 128), shaped(3, 17, 16, 256)),
        in_specs=[IN_SMEM, IN_VMEM],
        out_specs=(IN_VMEM,) * 4,
        scratch_shapes=[scratch(6, 17, 16, 256)] + [scratch(3, 17, 16, 256)] * 5,
        **PARAMS,
    )(moduli, ext)


def call_b(got):
    one, two = (3, 34, 16, 128), (3, 64, 128)
    return pl.pallas_call(
        kernel_b,
        out_shape=(shaped(2, 16, 128),) + (shaped(*one),) * 3 + (shaped(*two),) * 3,
        in_specs=[IN_VMEM],
        out_specs=(IN_VMEM,) * 7,
        scratch_shapes=[scratch(6, 34, 16, 128)] + [scratch(*one)] * 5,
        **PARAMS,
    )(got)


def call_c(place, got, level1, level2, level0):
    one, zero = (3, 34, 16, 128), (3, 17, 16, 256)
    return pl.pallas_call(
        kernel_c,
        out_shape=(shaped(3, 8, 8, 128), shaped(3, 8, 8, 128)),
        in_specs=[IN_SMEM] + [IN_VMEM] * 10,
        out_specs=(IN_VMEM,) * 2,
        scratch_shapes=[scratch(3, 5, 16, 128)] + [scratch(3, 256, 128)] * 3
        + [scratch(5, 256, 128), scratch(3, 448, 8, 128), scratch(272, 128), scratch(*one)]
        + [scratch(6, 34, 16, 128)] + [scratch(*one)] * 5
        + [scratch(6, 17, 16, 256)] + [scratch(*zero)] * 5,
        **PARAMS,
    )(place, got, *level1, *level2, *level0)


def both_ways(to_next, to_before, axis):
    count = lax.axis_size(axis)
    up = [(i, i + 1) for i in range(count - 1)]
    down = [(j, i) for i, j in up]
    return lax.ppermute(to_next, axis, up), lax.ppermute(to_before, axis, down)


def extend(body_forces, material, fixed_mask):
    cells = jnp.concatenate(
        [body_forces, (material + 1).astype(F32)[None], (1 - fixed_mask).astype(F32)[None]], axis=0
    )
    before, after = both_ways(cells, cells, "gz")
    halo = jnp.where(iota((1, 1, 1, 128), 3) < 64, after, before)
    cells = jnp.concatenate([cells, halo], axis=3)
    return wider(cells, 4)


def wider(cells, planes):
    before, after = both_ways(cells[:, 8 - planes : 8], cells[:, 0:planes], "gx")
    cells = jnp.concatenate([before, cells, after], axis=1)
    before, after = both_ways(cells[:, :, 4:8], cells[:, :, 0:4], "gy")
    return jnp.concatenate([cells, after, before], axis=2)


def to_all(block, axes, count):
    copies = jnp.broadcast_to(block[None], (count,) + block.shape)
    return lax.all_to_all(copies, axes, 0, 0, tiled=True)


def body(body_forces, material, fixed_mask, moduli):
    ext = extend(body_forces, material, fixed_mask)
    send, r0, x0, mod0 = call_a(moduli, ext)
    send, mod1, x1, r1, mod2, x2, r2 = call_b(to_all(send, ("gx", "gy"), 32))
    got = to_all(send, "gz", 16)
    place = jnp.stack([lax.axis_index("gx"), lax.axis_index("gy"), lax.axis_index("gz")]).astype(jnp.int32)
    return call_c(place, got, (mod1, x1, r1), (mod2, x2, r2), (mod0, x0, wider(r0, 3)))


def solution(mesh):
    cells = P(None, "gx", "gy", "gz")
    part = P("gx", "gy", "gz")
    return jax.shard_map(
        body, mesh=mesh, in_specs=(cells, part, part, P()), out_specs=(cells, cells), check_vma=False
    )
```
